256 devices in a mesh: dp: 32 (over y_hi, z, core), tensor: 8 (over y_lo, x).
Axes of the slice: x: 4, y: 4 (y_hi: 2, y_lo: 2; y = y_hi * 2 + y_lo), z: 8, core: 2. Of those that a mesh axis runs over, the one named last changes fastest.
Arguments:
- tokens: bfloat16 [8192, 1024], P('dp'), may hold values from -6 to 6
- gain: float32 [1024], replicated, may hold values from 0.1 to 1.9
- w_query: bfloat16 [1024, 8192], P(None, 'tensor'), may hold values from -1 to 1, as said below
- w_key: bfloat16 [1024, 8192], P(None, 'tensor'), may hold values from -1 to 1, as said below
- w_value: bfloat16 [1024, 8192], P(None, 'tensor'), may hold values from -0.1875 to 0.1875
- w_output: bfloat16 [8192, 1024], P('tensor'), may hold values from -0.0625 to 0.0625
- encoder: bfloat16 [1024, 256], replicated, may hold values from -0.1875 to 0.1875
- decoder: bfloat16 [256, 1024], replicated, may hold values from -0.375 to 0.375
- cotangent: bfloat16 [8192, 1024], P('dp'), may hold values from -6 to 6
Outputs:
- output: bfloat16 [8192, 1024], P('dp')
- grad_input: bfloat16 [8192, 1024], P('dp')
- grad_gain: float32 [1024], P(('dp', 'tensor'))
- grad_query: float32 [1024, 8192], P('dp', 'tensor')
- grad_key: float32 [1024, 8192], P('dp', 'tensor')
- grad_value: float32 [1024, 8192], P('dp', 'tensor')
- grad_output: float32 [8192, 1024], P('tensor', 'dp')
- grad_encoder: float32 [1024, 256], P(('dp', 'tensor'))
- grad_decoder: float32 [256, 1024], P('dp')
The draws below stay inside these ranges and needn't reach their ends.
Inputs may be any that keep to these rules, and one draw needn't show every extreme that they name: `w_query`: independent entries, mean zero. `w_key`: independent entries, mean zero.
All inputs are finite; a program needn't handle non-finite values.
Results may differ from the reference program's by a relative error of at most 0.024.
Values may be sent and summed in bfloat16 or wider, within the bound.
No kernel may reach another device: no remote copies, remote signals or barrier semaphores. Data moves between devices by JAX's collectives and lax.ppermute only.
A program may use at most 128 MiB of HBM per device.

```python
import jax
import jax.numpy as jnp
from jax import lax

D = 1024
HEADS = 64
DK = 128
CODE = 256
SEQ_LEN = 256
TOKENS = 8192
N_DP = 32
N_TENSOR = 8


def head_scaled(key, top):
    first, second = jax.random.split(key)
    base = jax.random.truncated_normal(first, -4.0, 4.0, (D, HEADS * DK), jnp.float32) * D ** (-0.5)
    factor = jnp.exp(jax.random.uniform(second, (HEADS,), jnp.float32) * top)
    scaled = base * jnp.repeat(factor, DK)[None, :]
    return jnp.clip(scaled, -1.0, 1.0).astype(jnp.bfloat16)


def draw_w_query(key, part):
    key = jax.random.fold_in(key, 11)
    return head_scaled(key, 0.0)


def draw_w_key(key, part):
    key = jax.random.fold_in(key, 23)
    return head_scaled(key, 0.0)


def shard_levels(own_key, dims, pieces, smallest, top_value):
    level, own = 1.0, jax.random.fold_in(own_key, 6)
    for dim, shards_of in pieces:
        heights = jnp.exp(jax.random.uniform(jax.random.fold_in(own, dim), (shards_of,), jnp.float32, smallest / len(pieces), top_value / len(pieces)))
        level = level * jnp.repeat(heights, dims[dim] // shards_of).reshape([-1 if axis == dim else 1 for axis in range(len(dims))])
    return level


def bell_draw(own_key, shape, spread, most, shards=(), held_as=jnp.bfloat16):
    result = jax.random.normal(own_key, shape, jnp.float32) * spread
    if len(shards) > 0:
        result = shard_levels(own_key, shape, shards, -0.22, 0.18) * result
    return jnp.clip(result, min=-most, max=most).astype(held_as)


def setup_inputs(seed: int = 0) -> dict:
    streams_of = jax.random.split(jax.random.key(seed), 10)
    tokens = bell_draw(streams_of[0], (TOKENS, D), 1.0, 6.0, ((0, 32),))
    gain = jnp.clip(1.0 + 0.18 * jax.random.normal(streams_of[1], (D,), jnp.float32), 0.1, 1.9)
    w_query = draw_w_query(jax.random.fold_in(streams_of[9], 71), 0)
    w_key = draw_w_key(jax.random.fold_in(streams_of[9], 71), 0)
    w_value = bell_draw(streams_of[4], (D, HEADS * DK), D ** -0.5, 0.1875, ((1, 8),))
    w_output = bell_draw(streams_of[5], (HEADS * DK, D), (HEADS * DK) ** -0.5, 0.0625, ((0, 8),))
    encoder = bell_draw(streams_of[6], (D, CODE), D ** -0.5, 0.1875)
    decoder = bell_draw(streams_of[7], (CODE, D), CODE ** -0.5, 0.375)
    cotangent = bell_draw(streams_of[8], (TOKENS, D), 1.0, 6.0, ((0, 32),))
    return {"tokens": tokens, "gain": gain, "w_query": w_query, "w_key": w_key, "w_value": w_value, "w_output": w_output, "encoder": encoder, "decoder": decoder, "cotangent": cotangent}


def attend(query, key, value):
    scores = jnp.einsum('qhd,khd->hqk', query.astype(jnp.float32), key.astype(jnp.float32)) * DK ** (-0.5)
    causal = jnp.arange(SEQ_LEN)[:, None] >= jnp.arange(SEQ_LEN)[None, :]
    masked = jnp.where(causal[None], scores, -1e+30)
    top = lax.optimization_barrier(jnp.max(masked, axis=-1, keepdims=True))
    expo = jnp.exp(masked - top)
    probs = expo / lax.optimization_barrier(jnp.sum(expo, axis=-1, keepdims=True))
    return probs

def forward_one(packed):
    query, key, value = packed
    probs_low = attend(query, key, value).astype(jnp.bfloat16)
    context = jnp.einsum('hqk,khd->qhd', probs_low.astype(jnp.float32), value.astype(jnp.float32))
    return context.astype(jnp.bfloat16)

def backward_one(packed):
    query, key, value, dcontext = packed
    probs = attend(query, key, value)
    probs_low = probs.astype(jnp.bfloat16)
    dfloat = dcontext.astype(jnp.float32)
    dprobs = jnp.einsum('qhd,khd->hqk', dfloat, value.astype(jnp.float32))
    dvalue = jnp.einsum('hqk,qhd->khd', probs_low.astype(jnp.float32), dfloat).astype(jnp.bfloat16)
    delta = lax.optimization_barrier(jnp.sum(dprobs * probs, axis=-1, keepdims=True))
    dscores = (probs * (dprobs - delta) * DK ** (-0.5)).astype(jnp.bfloat16).astype(jnp.float32)
    dquery = jnp.einsum('hqk,khd->qhd', dscores, key.astype(jnp.float32)).astype(jnp.bfloat16)
    dkey = jnp.einsum('hqk,qhd->khd', dscores, query.astype(jnp.float32)).astype(jnp.bfloat16)
    return (dquery, dkey, dvalue)

def grouped(left, right):
    left_blocks = left.reshape(N_DP, -1, left.shape[1])
    right_blocks = right.reshape(N_DP, -1, right.shape[1])

    def step(carry, pair):
        term = jnp.dot(pair[0].T, pair[1], preferred_element_type=jnp.float32).astype(jnp.bfloat16)
        term = lax.optimization_barrier(term)
        return (carry + term.astype(jnp.float32), None)
    start = jnp.zeros((left.shape[1], right.shape[1]), jnp.float32)
    total, _ = lax.scan(step, start, (left_blocks, right_blocks))
    return total

def reference(tokens, gain, w_query, w_key, w_value, w_output, encoder, decoder, cotangent):
    rows = tokens.shape[0]
    seqs_all = rows // SEQ_LEN
    group_cols = HEADS * DK // N_TENSOR
    xfloat = tokens.astype(jnp.float32)
    rms = lax.rsqrt(lax.optimization_barrier(jnp.mean(xfloat * xfloat, axis=-1, keepdims=True)) + 1e-06)
    unit = xfloat * rms
    normed = (unit * gain).astype(jnp.bfloat16)
    query = jnp.dot(normed, w_query, preferred_element_type=jnp.float32).astype(jnp.bfloat16)
    key = jnp.dot(normed, w_key, preferred_element_type=jnp.float32).astype(jnp.bfloat16)
    value = jnp.dot(normed, w_value, preferred_element_type=jnp.float32).astype(jnp.bfloat16)

    def per_seq(a):
        return a.reshape(seqs_all, SEQ_LEN, HEADS, DK)
    context = lax.map(forward_one, (per_seq(query), per_seq(key), per_seq(value))).reshape(rows, HEADS * DK)
    ctx_groups = context.reshape(rows, N_TENSOR, group_cols).transpose(1, 0, 2)
    out_groups = w_output.reshape(N_TENSOR, group_cols, D)

    def code_step(carry, pair):
        partial_value = jnp.dot(pair[0], pair[1], preferred_element_type=jnp.float32).astype(jnp.bfloat16)
        return (carry + jnp.dot(partial_value, encoder, preferred_element_type=jnp.float32), None)
    code_sum, _ = lax.scan(code_step, jnp.zeros((rows, CODE), jnp.float32), (ctx_groups, out_groups))
    code = code_sum.astype(jnp.bfloat16)
    output = (xfloat + jnp.dot(code, decoder, preferred_element_type=jnp.float32)).astype(jnp.bfloat16)
    dcode = jnp.dot(cotangent, decoder.T, preferred_element_type=jnp.float32).astype(jnp.bfloat16)
    dpartial = jnp.dot(dcode, encoder.T, preferred_element_type=jnp.float32).astype(jnp.bfloat16)

    def enc_step(carry, pair):
        partial_value = jnp.dot(pair[0], pair[1], preferred_element_type=jnp.float32).astype(jnp.bfloat16)
        return (carry + jnp.dot(partial_value.T, dcode, preferred_element_type=jnp.float32), None)
    grad_encoder, _ = lax.scan(enc_step, jnp.zeros((D, CODE), jnp.float32), (ctx_groups, out_groups))
    dcontext = jnp.dot(dpartial, w_output.T, preferred_element_type=jnp.float32).astype(jnp.bfloat16)
    dquery, dkey, dvalue = lax.map(backward_one, (per_seq(query), per_seq(key), per_seq(value), per_seq(dcontext)))
    dquery = dquery.reshape(rows, HEADS * DK)
    dkey = dkey.reshape(rows, HEADS * DK)
    dvalue = dvalue.reshape(rows, HEADS * DK)
    dnormed = jnp.dot(dquery, w_query.T, preferred_element_type=jnp.float32)
    dnormed = dnormed + jnp.dot(dkey, w_key.T, preferred_element_type=jnp.float32)
    dnormed = dnormed + jnp.dot(dvalue, w_value.T, preferred_element_type=jnp.float32)
    dunit = dnormed * gain
    inner = lax.optimization_barrier(jnp.sum(dunit * unit, axis=-1, keepdims=True)) / D
    grad_input = (cotangent.astype(jnp.float32) + rms * (dunit - unit * inner)).astype(jnp.bfloat16)
    grad_gain = lax.optimization_barrier(jnp.sum(dnormed * unit, axis=0))
    grad_query = grouped(normed, dquery)
    grad_key = grouped(normed, dkey)
    grad_value = grouped(normed, dvalue)
    grad_output = grouped(context, dpartial)
    grad_decoder = grouped(code, cotangent)
    return (output, grad_input, grad_gain, grad_query, grad_key, grad_value, grad_output, grad_encoder, grad_decoder)
```

```python
import jax
import jax.numpy as jnp
import numpy as np
from jax import lax
from jax.experimental import pallas as pl
from jax.experimental.pallas import tpu as pltpu
from jax.sharding import Mesh
from jax.sharding import PartitionSpec as P

DK = 128
SEQ = 256
YH, Z, CORES, YL, X = 2, 8, 2, 2, 4
NT = YL * X
TP = ("yl", "x")
F32 = jnp.float32
BF16 = jnp.bfloat16
SWAP = [(0, 1), (1, 0)]


def dot(a, b, ca=1, cb=0):
    return lax.dot_general(a, b, (((ca,), (cb,)), ((), ())), preferred_element_type=F32)


def forward_kernel(
    core_ref,
    tok_own,
    tok_oth,
    gain,
    wq,
    wk,
    wv,
    wo,
    enc,
    dec,
    cot_own,
    cot_oth,
    buf,
    normed_t,
    q_out,
    k_out,
    ds_out,
    dv_out,
    code_out,
    norm_s,
    dcode_s,
    v_s,
    dctx_s,
    ctx_s,
):
    own = wq.shape[1]
    heads = own // DK
    rows = tok_own.shape[1] // (YH * Z)
    gz = own // 2 // Z
    for s, tok in enumerate((tok_own, tok_oth)):
        x = tok[...].astype(F32)
        rms = lax.rsqrt(jnp.mean(x * x, axis=-1, keepdims=True) + 1e-6)
        norm_s[s * SEQ : (s + 1) * SEQ, :] = (x * rms * gain[...]).astype(BF16)
    dcode_s[0:SEQ, :] = dot(cot_own[...], dec[...], 1, 1).astype(BF16)
    dcode_s[SEQ:, :] = dot(cot_oth[...], dec[...], 1, 1).astype(BF16)
    normed = norm_s[...]
    normed_t[...] = normed.T
    q_out[...] = dot(normed, wq[...]).astype(BF16)
    k_out[...] = dot(normed, wk[...]).astype(BF16)
    v_s[...] = dot(normed, wv[...]).astype(BF16)
    w2 = dot(wo[...], enc[...]).astype(BF16)
    dctx_s[...] = dot(dcode_s[...], w2, 1, 1).astype(BF16)
    scale = DK**-0.5
    row = lax.broadcasted_iota(jnp.int32, (SEQ, SEQ), 0)
    col = lax.broadcasted_iota(jnp.int32, (SEQ, SEQ), 1)
    causal = row >= col
    for s in range(2):
        for h in range(heads):
            at = (slice(s * SEQ, (s + 1) * SEQ), slice(h * DK, (h + 1) * DK))
            q, k, v, dctx = q_out[at], k_out[at], v_s[at], dctx_s[at]
            scores = jnp.where(causal, dot(q, k, 1, 1) * scale, -1e30)
            top = jnp.max(scores, axis=-1, keepdims=True)
            expo = jnp.exp(scores - top)
            probs = expo * (1.0 / jnp.sum(expo, axis=-1, keepdims=True))
            low = probs.astype(BF16)
            ctx_s[at] = dot(low, v).astype(BF16)
            dprobs = dot(dctx, v, 1, 1)
            dv_out[at] = dot(low, dctx, 0, 0).astype(BF16)
            delta = jnp.sum(dprobs * probs, axis=-1, keepdims=True)
            ds_out[s * heads + h] = (probs * (dprobs - delta) * scale).astype(BF16)
    code_out[...] = dot(ctx_s[...], w2)
    gv = dot(normed_t[...], dv_out[...]).astype(BF16)
    g = dot(ctx_s[...], dcode_s[...], 0, 0).astype(BF16)
    code = g.shape[1]
    for z in range(Z):
        for y in range(YH):
            at = (y * Z + z) * rows
            buf[z, y * rows : (y + 1) * rows, :] = gv[at : at + rows, :]
        buf[z, YH * rows :, 0:code] = g[z * gz : (z + 1) * gz, :]
        buf[z, YH * rows :, code:] = g[own // 2 + z * gz : own // 2 + (z + 1) * gz, :]


def backward_kernel(
    core_ref, normed_t, q_in, k_in, ds_in, dv, code, wq, wk, wv, buf, keep, send, dq_s, dk_s
):
    width = wq.shape[0]
    own = wq.shape[1]
    heads = own // DK
    rows = width // (YH * Z)
    for s in range(2):
        for h in range(heads):
            at = (slice(s * SEQ, (s + 1) * SEQ), slice(h * DK, (h + 1) * DK))
            ds = ds_in[s * heads + h]
            dq_s[at] = dot(ds, k_in[at]).astype(BF16)
            dk_s[at] = dot(ds, q_in[at], 0, 0).astype(BF16)
    for i, g_s in enumerate((dq_s, dk_s)):
        g = dot(normed_t[...], g_s[...]).astype(BF16)
        for z in range(Z):
            for y in range(YH):
                at = (y * Z + z) * rows
                buf[z, y * rows : (y + 1) * rows, i * own : (i + 1) * own] = g[at : at + rows, :]
    for s, out in enumerate((keep, send)):
        at = slice(s * SEQ, (s + 1) * SEQ)
        dn = dot(dq_s[at, :], wq[...], 1, 1)
        dn = dn + dot(dk_s[at, :], wk[...], 1, 1)
        dn = dn + dot(dv[at, :], wv[...], 1, 1)
        out[:, 0:width] = dn.astype(out.dtype)
        out[:, width:] = code[at, :].astype(out.dtype)


def whole(shape):
    return pl.BlockSpec(shape, lambda i, core: (0,) * len(shape))


def run_kernel(body, core, args, blocks, outs, scratch, flops):
    specs = [whole(a.shape) if b is None else b for a, b in zip(args, blocks, strict=True)]
    moved = sum(a.size * a.dtype.itemsize for a in (*args, *outs))
    return pl.pallas_call(
        body,
        grid_spec=pltpu.PrefetchScalarGridSpec(
            num_scalar_prefetch=1,
            grid=(1,),
            in_specs=specs,
            out_specs=[whole(o.shape) for o in outs],
            scratch_shapes=scratch,
        ),
        out_shape=outs,
        compiler_params=pltpu.CompilerParams(vmem_limit_bytes=56 * 1024 * 1024),
        cost_estimate=pl.CostEstimate(flops=flops, bytes_accessed=moved, transcendentals=0),
    )(core, *args)


def on_device(tokens, gain, w_query, w_key, w_value, w_output, encoder, decoder, cotangent):
    rows, width = tokens.shape
    own = w_query.shape[1] // CORES
    heads = own // DK
    code_w = encoder.shape[1]
    yh, z, c = lax.axis_index("yh"), lax.axis_index("z"), lax.axis_index("c")
    t = lax.axis_index("yl") * X + lax.axis_index("x")
    dp = (yh * Z + z) * CORES + c
    part = width // (YH * Z)
    fine = part // CORES
    sds = jax.ShapeDtypeStruct
    core = jnp.reshape(c, (1,)).astype(jnp.int32)

    tok_oth = lax.ppermute(tokens, "c", SWAP)
    cot_oth = lax.ppermute(cotangent, "c", SWAP)

    by_col = pl.BlockSpec((width, own), lambda i, core: (0, core[0]))
    by_row = pl.BlockSpec((own, width), lambda i, core: (core[0], 0))
    gz = own // 2 // Z
    buf_a, normed_t, query, key, dscores, dvalue, code_p = run_kernel(
        forward_kernel,
        core,
        (
            tokens,
            tok_oth,
            gain.reshape(1, width),
            w_query,
            w_key,
            w_value,
            w_output,
            encoder,
            decoder,
            cotangent,
            cot_oth,
        ),
        (None, None, None, by_col, by_col, by_col, by_row, None, None, None, None),
        (
            sds((Z, YH * part + gz, own), BF16),
            sds((width, 2 * SEQ), BF16),
            sds((2 * SEQ, own), BF16),
            sds((2 * SEQ, own), BF16),
            sds((2 * heads, SEQ, SEQ), BF16),
            sds((2 * SEQ, own), BF16),
            sds((2 * SEQ, code_w), F32),
        ),
        (
            pltpu.VMEM((2 * SEQ, width), BF16),
            pltpu.VMEM((2 * SEQ, code_w), BF16),
            pltpu.VMEM((2 * SEQ, own), BF16),
            pltpu.VMEM((2 * SEQ, own), BF16),
            pltpu.VMEM((2 * SEQ, own), BF16),
        ),
        5_000_000_000,
    )
    red_a = lax.psum_scatter(buf_a, "z", scatter_dimension=0, tiled=True)[0]

    buf_b, keep, send = run_kernel(
        backward_kernel,
        core,
        (normed_t, query, key, dscores, dvalue, code_p, w_query, w_key, w_value),
        (None, None, None, None, None, None, by_col, by_col, by_col),
        (
            sds((Z, YH * part, 2 * own), BF16),
            sds((SEQ, width + code_w), F32),
            sds((SEQ, width + code_w), BF16),
        ),
        (pltpu.VMEM((2 * SEQ, own), BF16), pltpu.VMEM((2 * SEQ, own), BF16)),
        3_000_000_000,
    )
    red_b = lax.psum_scatter(buf_b, "z", scatter_dimension=0, tiled=True)[0]

    both = (keep + lax.ppermute(send, "c", SWAP).astype(F32)).astype(BF16)
    piece = rows // NT
    got = lax.all_to_all(both.reshape(NT, piece, width + code_w), TP, 0, 0, tiled=True)
    total = jnp.sum(got.astype(F32), axis=0)
    dnormed = total[:, :width]
    x = lax.dynamic_slice_in_dim(tokens, t * piece, piece, 0).astype(F32)
    cot = lax.dynamic_slice_in_dim(cotangent, t * piece, piece, 0).astype(F32)
    rms = lax.rsqrt(jnp.mean(x * x, axis=-1, keepdims=True) + 1e-6)
    unit = x * rms
    dunit = dnormed * gain
    inner = jnp.sum(dunit * unit, axis=-1, keepdims=True) / width
    grad_rows = cot + rms * (dunit - unit * inner)
    gain_row = jnp.sum(dnormed * unit, axis=0)
    gain_by_t = gain_row.reshape(YH * Z * CORES, NT, width // (YH * Z * CORES * NT))
    gain_by_t = gain_by_t.transpose(1, 0, 2).reshape(NT, 1, -1)
    gain_w = gain_by_t.shape[2]
    first = jnp.concatenate([grad_rows, total[:, width:]], axis=1).astype(BF16)
    out_w = width + code_w
    second = jnp.pad(gain_by_t, ((0, 0), (0, 15), (0, out_w - gain_w))).astype(BF16)
    packed = jnp.concatenate(
        [jnp.broadcast_to(first[None], (NT, piece, out_w)), second], axis=1
    )
    got = lax.all_to_all(packed, TP, 0, 0, tiled=True)
    whole_rows = got[:, :piece].reshape(rows, out_w)
    grad_input = whole_rows[:, :width]
    code = whole_rows[:, width:]
    output = (tokens.astype(F32) + dot(code, decoder)).astype(BF16)
    gain_sum = jnp.sum(got[:, piece, :gain_w].astype(F32), axis=0).reshape(YH * Z, CORES, -1)
    gain_keep = lax.dynamic_index_in_dim(gain_sum, c, 1, keepdims=False)
    gain_send = lax.dynamic_index_in_dim(gain_sum, 1 - c, 1, keepdims=False)
    gain_keep = gain_keep + lax.ppermute(gain_send, "c", SWAP)

    code_oth = lax.ppermute(code, "c", SWAP)
    cols = width // NT
    cot_own_c = lax.dynamic_slice_in_dim(cotangent, t * cols, cols, 1)
    cot_oth_c = lax.dynamic_slice_in_dim(cot_oth, t * cols, cols, 1)
    dec_p = dot(code, cot_own_c, 0, 0) + dot(code_oth, cot_oth_c, 0, 0)
    dec_rows = code_w // (YH * Z * CORES)
    dec_p = dec_p.reshape(YH * Z, CORES, dec_rows, cols)
    dec_p = lax.dynamic_index_in_dim(dec_p, c, 1, keepdims=False)

    swap_rows = jnp.where(yh == 0, red_a[part : 2 * part], red_a[0:part])
    from_yh = lax.ppermute(jnp.concatenate([swap_rows, red_a[2 * part :]], axis=0), "yh", SWAP)
    mine = jnp.where(yh == 0, red_a[0:part], red_a[part : 2 * part])
    gv = (mine.astype(F32) + from_yh[:part].astype(F32)).astype(BF16)
    g = (red_a[2 * part :].astype(F32) + from_yh[part:].astype(F32)).astype(BF16)
    g = jnp.where(yh == 0, g[:, :code_w], g[:, code_w:])

    n_yz = YH * Z
    flat = jnp.concatenate(
        [
            jnp.broadcast_to(g.reshape(1, -1), (n_yz, gz * code_w)),
            dec_p.astype(BF16).reshape(n_yz, -1),
            jnp.pad(gain_keep, ((0, 0), (0, 128 - gain_keep.shape[1]))).astype(BF16),
        ],
        axis=1,
    )
    got = lax.all_to_all(flat, ("yh", "z"), 0, 0, tiled=True)
    g_size, d_size = gz * code_w, dec_rows * cols
    g_own = got[:, :g_size].reshape(own, code_w)
    tail = jnp.sum(got[:, g_size:].astype(F32), axis=0)
    dec_sum = tail[:d_size].reshape(dec_rows, cols)
    grad_gain = tail[d_size : d_size + gain_keep.shape[1]]
    g_oth = lax.ppermute(g_own, "c", SWAP)
    g_all = jnp.concatenate(
        [jnp.where(c == 0, g_own, g_oth), jnp.where(c == 0, g_oth, g_own)], axis=0
    )
    enc_rows = lax.dynamic_slice_in_dim(encoder, dp * fine, fine, 0)
    grad_output = dot(g_all, enc_rows, 1, 1)
    wo_cols = lax.dynamic_slice_in_dim(w_output, dp * fine, fine, 1)
    enc_p = dot(wo_cols, g_all, 0, 0)

    flat = jnp.concatenate(
        [
            jnp.broadcast_to(dec_sum.reshape(1, -1), (NT, d_size)),
            enc_p.reshape(NT, -1),
        ],
        axis=1,
    )
    got = lax.all_to_all(flat, TP, 0, 0, tiled=True)
    grad_decoder = got[:, :d_size].reshape(NT, dec_rows, cols).transpose(1, 0, 2)
    grad_decoder = grad_decoder.reshape(dec_rows, width)
    grad_encoder = jnp.sum(got[:, d_size:], axis=0).reshape(-1, code_w)

    swap_rows = jnp.where(yh == 0, red_b[part:], red_b[:part])
    mine = jnp.where(yh == 0, red_b[:part], red_b[part:])
    gqk = (mine.astype(F32) + lax.ppermute(swap_rows, "yh", SWAP).astype(F32)).astype(BF16)

    def over_cores(a):
        kept = jnp.where(c == 0, a[:fine], a[fine:])
        other = lax.ppermute(jnp.where(c == 0, a[fine:], a[:fine]), "c", SWAP)
        low = jnp.where(c == 0, kept, other).astype(F32)
        high = jnp.where(c == 0, other, kept).astype(F32)
        return low, high

    low, high = over_cores(gv)
    grad_value = jnp.concatenate([low, high], axis=1)
    low, high = over_cores(gqk)
    grad_query = jnp.concatenate([low[:, :own], high[:, :own]], axis=1)
    grad_key = jnp.concatenate([low[:, own:], high[:, own:]], axis=1)
    return (
        output,
        grad_input,
        grad_gain,
        grad_query,
        grad_key,
        grad_value,
        grad_output,
        grad_encoder,
        grad_decoder,
    )


def solution(mesh):
    devices = np.asarray(mesh.devices).reshape(YH, Z, CORES, YL, X)
    fine = Mesh(devices, ("yh", "z", "c", "yl", "x"))
    dp = ("yh", "z", "c")
    every = (*dp, *TP)
    return jax.shard_map(
        on_device,
        mesh=fine,
        in_specs=(
            P(dp, None),
            P(),
            P(None, TP),
            P(None, TP),
            P(None, TP),
            P(TP, None),
            P(),
            P(),
            P(dp, None),
        ),
        out_specs=(
            P(dp, None),
            P(dp, None),
            P(every),
            P(dp, TP),
            P(dp, TP),
            P(dp, TP),
            P(TP, dp),
            P(every, None),
            P(dp, None),
        ),
        check_vma=False,
    )
```

```python
import jax
import jax.numpy as jnp
import numpy as np
from jax import lax
from jax.experimental import pallas as pl
from jax.experimental.pallas import tpu as pltpu
from jax.sharding import Mesh
from jax.sharding import PartitionSpec as P

DK = 128
SEQ = 256
YH, Z, CORES, YL, X = 2, 8, 2, 2, 4
NT = YL * X
TP = ("yl", "x")
F32 = jnp.float32
BF16 = jnp.bfloat16
SWAP = [(0, 1), (1, 0)]


def dot(a, b, ca=1, cb=0):
    return lax.dot_general(a, b, (((ca,), (cb,)), ((), ())), preferred_element_type=F32)


def block_kernel(
    core_ref,
    gain,
    tok_own_h,
    tok_oth_h,
    wq_h,
    cot_own_h,
    cot_oth_h,
    dec_h,
    wo_h,
    enc_h,
    wk_h,
    wv_h,
    buf_h,
    send,
    keep,
    enc_out,
    tok,
    cot,
    wq,
    wk,
    wv,
    wo,
    enc,
    dec,
    norm_s,
    norm_t,
    dcode_s,
    q_s,
    k_s,
    v_s,
    dctx_s,
    ctx_s,
    dq_s,
    dk_s,
    dv_s,
    stage,
    in_sem,
    out_sem,
):
    width, own = wq.shape
    heads = own // DK
    code = enc.shape[1]
    part = width // (YH * Z)
    core = core_ref[0]
    mine = pl.ds(pl.multiple_of(core * own, own), own)
    pairs = (
        (tok_own_h, tok.at[pl.ds(0, SEQ)]),
        (tok_oth_h, tok.at[pl.ds(SEQ, SEQ)]),
        (wq_h.at[:, mine], wq),
        (wk_h.at[:, mine], wk),
        (wv_h.at[:, mine], wv),
        (cot_own_h, cot.at[pl.ds(0, SEQ)]),
        (cot_oth_h, cot.at[pl.ds(SEQ, SEQ)]),
        (dec_h, dec),
        (wo_h.at[mine, :], wo),
        (enc_h, enc),
    )
    copies = [pltpu.make_async_copy(a, b, in_sem.at[i]) for i, (a, b) in enumerate(pairs)]
    for copy in copies:
        copy.start()

    for s in range(2):
        at = slice(s * SEQ, (s + 1) * SEQ)
        copies[s].wait()
        x = tok[at, :].astype(F32)
        rms = lax.rsqrt(jnp.mean(x * x, axis=-1, keepdims=True) + 1e-6)
        norm_s[at, :] = (x * rms * gain[...]).astype(BF16)
    normed = norm_s[...]
    copies[2].wait()
    q_s[...] = dot(normed, wq[...]).astype(BF16)
    norm_t[...] = normed.T
    copies[3].wait()
    k_s[...] = dot(normed, wk[...]).astype(BF16)
    copies[4].wait()
    v_s[...] = dot(normed, wv[...]).astype(BF16)
    for copy in copies[5:]:
        copy.wait()
    dcode_s[...] = dot(cot[...], dec[...], 1, 1).astype(BF16)
    w2 = dot(wo[...], enc[...]).astype(BF16)
    dctx_s[...] = dot(dcode_s[...], w2, 1, 1).astype(BF16)
    scale = DK**-0.5
    row = lax.broadcasted_iota(jnp.int32, (SEQ, SEQ), 0)
    col = lax.broadcasted_iota(jnp.int32, (SEQ, SEQ), 1)
    causal = row >= col
    for s in range(2):
        for h in range(heads):
            at = (slice(s * SEQ, (s + 1) * SEQ), slice(h * DK, (h + 1) * DK))
            q, k, v, dctx = q_s[at], k_s[at], v_s[at], dctx_s[at]
            scores = jnp.where(causal, dot(q, k, 1, 1) * scale, -1e30)
            top = jnp.max(scores, axis=-1, keepdims=True)
            expo = jnp.exp(scores - top)
            probs = expo * (1.0 / jnp.sum(expo, axis=-1, keepdims=True))
            low = probs.astype(BF16)
            ctx_s[at] = dot(low, v).astype(BF16)
            dprobs = dot(dctx, v, 1, 1)
            dv_s[at] = dot(low, dctx, 0, 0).astype(BF16)
            delta = jnp.sum(dprobs * probs, axis=-1, keepdims=True)
            ds = (probs * (dprobs - delta) * scale).astype(BF16)
            dq_s[at] = dot(ds, k).astype(BF16)
            dk_s[at] = dot(ds, q, 0, 0).astype(BF16)

    def put(i, g):
        lanes = slice(i * own, (i + 1) * own)
        for z in range(Z):
            for y in range(YH):
                at = (y * Z + z) * part
                stage[z, y * part : (y + 1) * part, lanes] = g[at : at + part, :].astype(BF16)
        there = buf_h.at[:, :, pl.ds(i * own, own)]
        copy = pltpu.make_async_copy(stage.at[:, :, pl.ds(i * own, own)], there, out_sem.at[i])
        copy.start()
        return copy

    g = dot(ctx_s[...], dcode_s[...], 0, 0).astype(BF16)
    out = [put(3, dot(enc[...], g, 1, 1))]
    out.append(put(2, dot(norm_t[...], dv_s[...])))
    out.append(put(0, dot(norm_t[...], dq_s[...])))
    out.append(put(1, dot(norm_t[...], dk_s[...])))
    for s, ref in enumerate((keep, send)):
        at = slice(s * SEQ, (s + 1) * SEQ)
        dn = dot(dq_s[at, :], wq[...], 1, 1)
        dn = dn + dot(dk_s[at, :], wk[...], 1, 1)
        dn = dn + dot(dv_s[at, :], wv[...], 1, 1)
        ref[:, 0:width] = dn.astype(BF16)
        ref[:, width : width + code] = dot(ctx_s[at, :], w2).astype(BF16)
    enc_out[...] = dot(wo[...], g, 0, 0).astype(BF16)
    for copy in out:
        copy.wait()


def run_block(core, gain, *args):
    tokens, wq, enc = args[0], args[2], args[7]
    width, own = wq.shape[0], wq.shape[1] // CORES
    code = enc.shape[1]
    part = width // (YH * Z)
    sds = jax.ShapeDtypeStruct
    outs = (
        sds((Z, YH * part, 4 * own), BF16),
        sds((SEQ, width + code), BF16),
        sds((SEQ, width + code), BF16),
        sds((width, code), BF16),
    )
    vmem = pl.BlockSpec(memory_space=pltpu.VMEM)
    hbm = pl.BlockSpec(memory_space=pl.ANY)
    two = 2 * SEQ
    shapes = (
        (two, width),
        (two, width),
        (width, own),
        (width, own),
        (width, own),
        (own, width),
        (width, code),
        (code, width),
        (two, width),
        (width, two),
        (two, code),
        *(((two, own),) * 8),
        (Z, YH * part, 4 * own),
    )
    return pl.pallas_call(
        block_kernel,
        in_specs=[pl.BlockSpec(memory_space=pltpu.SMEM), vmem, *([hbm] * len(args))],
        out_specs=[hbm, vmem, vmem, vmem],
        out_shape=outs,
        scratch_shapes=[
            *(pltpu.VMEM(shape, BF16) for shape in shapes),
            pltpu.SemaphoreType.DMA((10,)),
            pltpu.SemaphoreType.DMA((4,)),
        ],
        compiler_params=pltpu.CompilerParams(vmem_limit_bytes=56 * 1024 * 1024),
        cost_estimate=pl.CostEstimate(
            flops=7_500_000_000, bytes_accessed=14_000_000, transcendentals=600_000
        ),
    )(core, gain, *args)


def on_device(tokens, gain, w_query, w_key, w_value, w_output, encoder, decoder, cotangent):
    rows, width = tokens.shape
    own = w_query.shape[1] // CORES
    code_w = encoder.shape[1]
    yh, z, c = lax.axis_index("yh"), lax.axis_index("z"), lax.axis_index("c")
    t = lax.axis_index("yl") * X + lax.axis_index("x")
    n_yz = YH * Z
    n_dp = n_yz * CORES
    fine = width // n_dp
    tiny = fine // NT
    core = jnp.reshape(c, (1,)).astype(jnp.int32)

    tok_oth = lax.ppermute(tokens, "c", SWAP)
    cot_oth = lax.ppermute(cotangent, "c", SWAP)
    buf, send, keep, enc_p = run_block(
        core,
        gain.reshape(1, width),
        tokens,
        tok_oth,
        w_query,
        cotangent,
        cot_oth,
        decoder,
        w_output,
        encoder,
        w_key,
        w_value,
    )
    red = lax.psum_scatter(buf, "z", scatter_dimension=0, tiled=True)

    both = (keep.astype(F32) + lax.ppermute(send, "c", SWAP).astype(F32)).astype(BF16)
    piece = rows // NT
    got = lax.all_to_all(both.reshape(NT, piece, width + code_w), TP, 0, 0, tiled=True)
    total = jnp.sum(got.astype(F32), axis=0)
    dnormed = total[:, :width]
    x = lax.dynamic_slice_in_dim(tokens, t * piece, piece, 0).astype(F32)
    cot = lax.dynamic_slice_in_dim(cotangent, t * piece, piece, 0).astype(F32)
    rms = lax.rsqrt(jnp.mean(x * x, axis=-1, keepdims=True) + 1e-6)
    unit = x * rms
    dunit = dnormed * gain
    inner = jnp.sum(dunit * unit, axis=-1, keepdims=True) / width
    grad_rows = cot + rms * (dunit - unit * inner)
    gain_row = jnp.sum(dnormed * unit, axis=0)
    gain_by_t = gain_row.reshape(n_dp, NT, tiny).transpose(1, 0, 2).reshape(NT, 1, -1)
    gain_w = n_dp * tiny

    enc_p = enc_p.reshape(n_yz, CORES, fine, code_w)
    enc_keep = lax.dynamic_index_in_dim(enc_p, c, 1, keepdims=False)
    enc_send = lax.dynamic_index_in_dim(enc_p, 1 - c, 1, keepdims=False)
    enc_c = enc_keep.astype(F32) + lax.ppermute(enc_send, "c", SWAP).astype(F32)
    enc_c = enc_c.astype(BF16).reshape(n_yz, NT, tiny, code_w).transpose(1, 0, 2, 3)
    enc_c = enc_c.reshape(NT, n_yz * tiny, code_w)

    first = jnp.concatenate([grad_rows, total[:, width:]], axis=1).astype(BF16)
    out_w = width + code_w
    half = n_yz * tiny // 2
    enc_c = jnp.concatenate([enc_c[:, :half], enc_c[:, half:]], axis=2)
    enc_c = jnp.pad(enc_c, ((0, 0), (0, piece - half), (0, 0)))
    gain_b = jnp.pad(gain_by_t, ((0, 0), (0, piece - 1), (0, -gain_w % 128))).astype(BF16)
    packed = jnp.concatenate(
        [jnp.broadcast_to(first[None], (NT, piece, out_w)), enc_c, gain_b], axis=2
    )
    got = lax.all_to_all(packed, TP, 0, 0, tiled=True)
    whole_rows = got[:, :, :out_w].reshape(rows, out_w)
    grad_input = whole_rows[:, :width]
    code = whole_rows[:, width:]
    code_oth = lax.ppermute(code, "c", SWAP)
    sums = jnp.sum(got[:, :, out_w:].astype(F32), axis=0)
    enc_t = jnp.concatenate(
        [sums[:half, :code_w], sums[:half, code_w : 2 * code_w]], axis=0
    ).reshape(n_yz, -1)
    gain_sum = sums[0, 2 * code_w : 2 * code_w + gain_w].reshape(n_yz, CORES, tiny)
    gain_keep = lax.dynamic_index_in_dim(gain_sum, c, 1, keepdims=False)
    gain_send = lax.dynamic_index_in_dim(gain_sum, 1 - c, 1, keepdims=False)
    gain_keep = gain_keep + lax.ppermute(gain_send, "c", SWAP)

    cols = width // NT
    cot_own_c = lax.dynamic_slice_in_dim(cotangent, t * cols, cols, 1)
    cot_oth_c = lax.dynamic_slice_in_dim(cot_oth, t * cols, cols, 1)
    dec_p = dot(code, cot_own_c, 0, 0) + dot(code_oth, cot_oth_c, 0, 0)
    dec_rows = code_w // n_dp
    dec_p = dec_p.reshape(n_yz, CORES, dec_rows, cols)
    dec_p = lax.dynamic_index_in_dim(dec_p, c, 1, keepdims=False)

    flat = jnp.concatenate(
        [
            dec_p.reshape(n_yz, -1),
            enc_t,
            jnp.pad(gain_keep, ((0, 0), (0, 128 - tiny))),
        ],
        axis=1,
    ).astype(BF16)
    got = lax.all_to_all(flat, ("yh", "z"), 0, 0, tiled=True)
    tail = jnp.sum(got.astype(F32), axis=0)
    d_size, e_size = dec_rows * cols, tiny * code_w
    grad_encoder = tail[d_size : d_size + e_size].reshape(tiny, code_w)
    grad_gain = tail[d_size + e_size : d_size + e_size + tiny]
    dec_sum = jnp.broadcast_to(tail[:d_size].reshape(1, dec_rows, cols), (NT, dec_rows, cols))
    got = lax.all_to_all(dec_sum, TP, 0, 0, tiled=True)
    grad_decoder = got.transpose(1, 0, 2).reshape(dec_rows, width)
    output = (tokens.astype(F32) + dot(code, decoder)).astype(BF16)

    got = lax.all_to_all(
        red.reshape(YH * CORES, fine, 4 * own), ("yh", "c"), 0, 0, tiled=True
    )
    got = got.reshape(YH, CORES, fine, 4, own).astype(F32)
    grads = got[0] + got[1]
    grads = [
        jnp.concatenate([grads[0, :, i], grads[1, :, i]], axis=1) for i in range(4)
    ]
    return (
        output,
        grad_input,
        grad_gain,
        grads[0],
        grads[1],
        grads[2],
        grads[3].T,
        grad_encoder,
        grad_decoder,
    )


def solution(mesh):
    devices = np.asarray(mesh.devices).reshape(YH, Z, CORES, YL, X)
    fine = Mesh(devices, ("yh", "z", "c", "yl", "x"))
    dp = ("yh", "z", "c")
    every = (*dp, *TP)
    return jax.shard_map(
        on_device,
        mesh=fine,
        in_specs=(
            P(dp, None),
            P(),
            P(None, TP),
            P(None, TP),
            P(None, TP),
            P(TP, None),
            P(),
            P(),
            P(dp, None),
        ),
        out_specs=(
            P(dp, None),
            P(dp, None),
            P(every),
            P(dp, TP),
            P(dp, TP),
            P(dp, TP),
            P(TP, dp),
            P(every, None),
            P(dp, None),
        ),
        check_vma=False,
    )
```

```python
import functools

import jax
import jax.numpy as jnp
import numpy as np
from jax import lax
from jax.experimental import pallas as pl
from jax.experimental.pallas import tpu as pltpu
from jax.sharding import Mesh
from jax.sharding import PartitionSpec as P

DK = 128
SEQ = 256
YH, Z, CORES, YL, X = 2, 8, 2, 2, 4
NT = YL * X
TP = ("yl", "x")
F32 = jnp.float32
BF16 = jnp.bfloat16
SWAP = [(0, 1), (1, 0)]


def dot(a, b, ca=1, cb=0):
    return lax.dot_general(a, b, (((ca,), (cb,)), ((), ())), preferred_element_type=F32)


def block_kernel(
    core_ref,
    gain,
    tok_own_h,
    tok_oth_h,
    wq_h,
    cot_own_h,
    cot_oth_h,
    dec_h,
    wo_h,
    enc_h,
    wk_h,
    wv_h,
    buf_h,
    keep,
    send,
    first,
    tok,
    cot,
    wq,
    wk,
    wv,
    wo,
    enc,
    dec,
    norm_s,
    norm_t,
    dcode_s,
    q_s,
    k_s,
    v_s,
    dctx_s,
    ctx_s,
    dq_s,
    dk_s,
    dv_s,
    code_s,
    stage,
    rms_s,
    enc_s,
    small_s,
    in_sem,
    out_sem,
):
    width, own = wq.shape
    heads = own // DK
    code = enc.shape[1]
    part = width // (YH * Z)
    core = core_ref[0]
    far = lax.rem(core_ref[1] + Z // 2, Z)
    mine = pl.ds(pl.multiple_of(core * own, own), own)
    pairs = (
        (tok_own_h, tok.at[pl.ds(0, SEQ)]),
        (tok_oth_h, tok.at[pl.ds(SEQ, SEQ)]),
        (wq_h.at[:, mine], wq),
        (wk_h.at[:, mine], wk),
        (wv_h.at[:, mine], wv),
        (cot_own_h, cot.at[pl.ds(0, SEQ)]),
        (cot_oth_h, cot.at[pl.ds(SEQ, SEQ)]),
        (dec_h, dec),
        (wo_h.at[mine, :], wo),
        (enc_h, enc),
    )
    copies = [pltpu.make_async_copy(a, b, in_sem.at[i]) for i, (a, b) in enumerate(pairs)]
    for copy in copies:
        copy.start()

    for s in range(2):
        at = slice(s * SEQ, (s + 1) * SEQ)
        copies[s].wait()
        x = tok[at, :].astype(F32)
        rms = lax.rsqrt(jnp.mean(x * x, axis=-1, keepdims=True) + 1e-6)
        rms_s[at, :] = jnp.broadcast_to(rms, (SEQ, 128))
        norm_s[at, :] = (x * rms * gain[...]).astype(BF16)
    normed = norm_s[...]
    copies[2].wait()
    q_s[...] = dot(normed, wq[...]).astype(BF16)
    norm_t[...] = normed.T
    copies[3].wait()
    k_s[...] = dot(normed, wk[...]).astype(BF16)
    copies[4].wait()
    v_s[...] = dot(normed, wv[...]).astype(BF16)
    for copy in copies[5:]:
        copy.wait()
    dcode_s[...] = dot(cot[...], dec[...], 1, 1).astype(BF16)
    w2 = dot(wo[...], enc[...]).astype(BF16)
    dctx_s[...] = dot(dcode_s[...], w2, 1, 1).astype(BF16)
    scale = DK**-0.5
    row = lax.broadcasted_iota(jnp.int32, (SEQ, SEQ), 0)
    col = lax.broadcasted_iota(jnp.int32, (SEQ, SEQ), 1)
    causal = row >= col
    for s in range(2):
        for h in range(heads):
            at = (slice(s * SEQ, (s + 1) * SEQ), slice(h * DK, (h + 1) * DK))
            q, k, v, dctx = q_s[at], k_s[at], v_s[at], dctx_s[at]
            scores = jnp.where(causal, dot(q, k, 1, 1) * scale, -1e30)
            top = jnp.max(scores, axis=-1, keepdims=True)
            expo = jnp.exp(scores - top)
            probs = expo * (1.0 / jnp.sum(expo, axis=-1, keepdims=True))
            low = probs.astype(BF16)
            ctx_s[at] = dot(low, v).astype(BF16)
            dprobs = dot(dctx, v, 1, 1)
            dv_s[at] = dot(low, dctx, 0, 0).astype(BF16)
            delta = jnp.sum(dprobs * probs, axis=-1, keepdims=True)
            ds = (probs * (dprobs - delta) * scale).astype(BF16)
            dq_s[at] = dot(ds, k).astype(BF16)
            dk_s[at] = dot(ds, q, 0, 0).astype(BF16)

    def put(i, g):
        lanes = slice(i * own, (i + 1) * own)
        for z in range(Z):
            for y in range(YH):
                at = (y * Z + z) * part
                stage[z, y * part : (y + 1) * part, lanes] = g[at : at + part, :].astype(BF16)
        there = buf_h.at[:, :, pl.ds(i * own, own)]
        copy = pltpu.make_async_copy(stage.at[:, :, pl.ds(i * own, own)], there, out_sem.at[i])
        copy.start()
        return copy

    g = dot(ctx_s[...], dcode_s[...], 0, 0).astype(BF16)
    out = [put(3, dot(enc[...], g, 1, 1))]
    out.append(put(2, dot(norm_t[...], dv_s[...])))
    out.append(put(0, dot(norm_t[...], dq_s[...])))
    out.append(put(1, dot(norm_t[...], dk_s[...])))
    for i in range(2):
        half = YH * part // 2
        first[i] = stage[far, i * half : (i + 1) * half, :]
    piece = SEQ // NT
    code_s[...] = dot(ctx_s[...], w2).astype(BF16)
    gain_p = jnp.zeros((1, width), F32)
    for s in range(2):
        at = slice(s * SEQ, (s + 1) * SEQ)
        dn = dot(dq_s[at, :], wq[...], 1, 1)
        dn = dn + dot(dk_s[at, :], wk[...], 1, 1)
        dn = dn + dot(dv_s[at, :], wv[...], 1, 1)
        unit = tok[at, :].astype(F32) * rms_s[at, 0:1]
        gain_p = gain_p + jnp.sum(dn * unit, axis=0, keepdims=True)
        low = dn.astype(BF16)
        for t in range(NT):
            here = slice(t * piece, (t + 1) * piece)
            there = slice(s * SEQ + t * piece, s * SEQ + (t + 1) * piece)
            ref = (keep, send)[s]
            ref[t, :, 0:width] = low[here, :]
            ref[t, :, width : width + code] = code_s[there, :]
    enc_s[...] = dot(wo[...], g, 0, 0)
    dec_p = dot(code_s[...], cot[...], 0, 0).astype(BF16)
    n_yz = YH * Z
    fine = part // CORES
    tiny = fine // NT
    rows = code // n_yz // CORES
    cols = width // NT
    blocks = n_yz * rows // piece
    each = piece // rows
    base = width + code
    for cc in range(CORES):
        small = small_s.at[jnp.where(core == cc, 0, 1)]
        for t in range(NT):
            for j in range(blocks):
                dec_at = j * 2 * cols
                dec_b, enc_b = [], []
                for yz in range(j * each, (j + 1) * each):
                    r = (yz * CORES + cc) * rows
                    dec_b.append(dec_p[r : r + rows, t * cols : (t + 1) * cols])
                    e = (yz * CORES + cc) * fine + t * tiny
                    enc_b.append(enc_s[e : e + tiny, 0:cols])
                    enc_b.append(enc_s[e : e + tiny, cols : 2 * cols])
                small[t, :, dec_at : dec_at + cols] = jnp.concatenate(dec_b, axis=0)
                enc_v = jnp.concatenate(enc_b, axis=0).astype(BF16)
                small[t, :, dec_at + cols : dec_at + 2 * cols] = enc_v
    gain_v = jnp.concatenate(
        [gain_p[:, i * 128 : (i + 1) * 128] for i in range(width // 128)]
        + [jnp.zeros((piece - width // 128, 128), F32)],
        axis=0,
    ).astype(BF16)
    end = base + blocks * 2 * cols
    for s, ref in enumerate((keep, send)):
        ref[:, :, base:end] = small_s[s]
        for t in range(NT):
            ref[t, :, end:] = gain_v
    for copy in out:
        copy.wait()


def run_block(core, gain, *args):
    tokens, wq, enc = args[0], args[2], args[7]
    width, own = wq.shape[0], wq.shape[1] // CORES
    code = enc.shape[1]
    part = width // (YH * Z)
    sds = jax.ShapeDtypeStruct
    piece = SEQ // NT
    lanes = width + code + width + 128
    outs = (
        sds((Z, YH * part, 4 * own), BF16),
        sds((NT, piece, lanes), BF16),
        sds((NT, piece, lanes), BF16),
        sds((2, YH * part // 2, 4 * own), BF16),
    )
    vmem = pl.BlockSpec(memory_space=pltpu.VMEM)
    hbm = pl.BlockSpec(memory_space=pl.ANY)
    two = 2 * SEQ
    shapes = (
        (two, width),
        (two, width),
        (width, own),
        (width, own),
        (width, own),
        (own, width),
        (width, code),
        (code, width),
        (two, width),
        (width, two),
        (two, code),
        *(((two, own),) * 8),
        (two, code),
        (Z, YH * part, 4 * own),
    )
    return pl.pallas_call(
        block_kernel,
        in_specs=[pl.BlockSpec(memory_space=pltpu.SMEM), vmem, *([hbm] * len(args))],
        out_specs=[hbm, vmem, vmem, vmem],
        out_shape=outs,
        scratch_shapes=[
            *(pltpu.VMEM(shape, BF16) for shape in shapes),
            pltpu.VMEM((two, 128), F32),
            pltpu.VMEM((width, code), F32),
            pltpu.VMEM((2, NT, piece, width), BF16),
            pltpu.SemaphoreType.DMA((10,)),
            pltpu.SemaphoreType.DMA((4,)),
        ],
        compiler_params=pltpu.CompilerParams(vmem_limit_bytes=56 * 1024 * 1024),
        cost_estimate=pl.CostEstimate(
            flops=7_500_000_000, bytes_accessed=14_000_000, transcendentals=600_000
        ),
    )(core, gain, *args)


def ring_chunk(buf, z, c, k, sign):
    turn = k * sign * (1 - 2 * c)
    return lax.dynamic_index_in_dim(buf, lax.rem(z + turn + Z, Z), 0, keepdims=False)


def ring_send(held):
    return [
        lax.ppermute(
            a,
            ("z", "c"),
            [
                (at * CORES + core, (at + sign * (1 - 2 * core)) % Z * CORES + core)
                for at in range(Z)
                for core in range(CORES)
            ],
        )
        for a, sign in zip(held, (1, -1), strict=True)
    ]


def ring_add(chunk, k, got):
    out = []
    for a, sign in zip(got, (1, -1), strict=True):
        local = chunk(k, sign)
        half = local.shape[0] // 2
        if k < Z // 2 - 1:
            out.append((local.astype(F32) + a.astype(F32)).astype(BF16))
            continue
        rows = slice(0, half) if sign == 1 else slice(half, 2 * half)
        added = (local[rows].astype(F32) + a.astype(F32)).astype(BF16)
        parts = [added, local[half:]] if sign == 1 else [local[:half], added]
        out.append(jnp.concatenate(parts, axis=0))
    return out


def on_device(tokens, gain, w_query, w_key, w_value, w_output, encoder, decoder, cotangent):
    rows, width = tokens.shape
    own = w_query.shape[1] // CORES
    code_w = encoder.shape[1]
    yh, z, c = lax.axis_index("yh"), lax.axis_index("z"), lax.axis_index("c")
    t = lax.axis_index("yl") * X + lax.axis_index("x")
    n_dp = YH * Z * CORES
    fine = width // n_dp
    tiny = fine // NT
    core = jnp.stack([c, z]).astype(jnp.int32)

    tok_oth = lax.ppermute(tokens, "c", SWAP)
    cot_oth = lax.ppermute(cotangent, "c", SWAP)
    buf, keep, send, first = run_block(
        core,
        gain.reshape(1, width),
        tokens,
        tok_oth,
        w_query,
        cotangent,
        cot_oth,
        decoder,
        w_output,
        encoder,
        w_key,
        w_value,
    )
    chunk = functools.partial(ring_chunk, buf, z, c)
    got = ring_send([first[0], first[1]])
    both = (keep.astype(F32) + lax.ppermute(send, "c", SWAP).astype(F32)).astype(BF16)
    *got, both = lax.optimization_barrier((*got, both))

    over_t = lax.all_to_all(both, TP, 0, 0, tiled=True)
    got = ring_send(ring_add(chunk, 3, got))
    *got, over_t = lax.optimization_barrier((*got, over_t))

    total = jnp.sum(over_t.astype(F32), axis=0)
    piece = rows // NT
    out_w = width + code_w
    cols = width // NT
    dec_rows = code_w // n_dp
    small = total[:, out_w : out_w + width]
    small = jnp.concatenate(
        [small[:, i * 2 * cols : (i + 1) * 2 * cols] for i in range(width // (2 * cols))], axis=0
    ).reshape(YH * Z, dec_rows, 2 * cols)
    gain_v = total[: width // 128, out_w + width :]
    small = jnp.concatenate(
        [small, jnp.broadcast_to(gain_v[None], (YH * Z, *gain_v.shape))], axis=2
    ).astype(BF16)
    small = lax.all_to_all(small, ("yh", "z"), 0, 0, tiled=True)
    got = ring_send(ring_add(chunk, 2, got))

    dnormed = total[:, :width]
    x = lax.dynamic_slice_in_dim(tokens, t * piece, piece, 0).astype(F32)
    cot = lax.dynamic_slice_in_dim(cotangent, t * piece, piece, 0).astype(F32)
    rms = lax.rsqrt(jnp.mean(x * x, axis=-1, keepdims=True) + 1e-6)
    unit = x * rms
    dunit = dnormed * gain
    inner = jnp.sum(dunit * unit, axis=-1, keepdims=True) / width
    grad_rows = cot + rms * (dunit - unit * inner)
    mine = jnp.concatenate([grad_rows, total[:, width:out_w]], axis=1).astype(BF16)
    *got, small, mine = lax.optimization_barrier((*got, small, mine))

    small = jnp.sum(small.astype(F32), axis=0)
    enc_v = small[:, cols : 2 * cols]
    grad_encoder = jnp.concatenate([enc_v[:tiny], enc_v[tiny:]], axis=1)
    at = (((yh * Z + z) * CORES + c) * NT + t) * tiny
    grad_gain = lax.dynamic_slice(small, (at // 128, 2 * cols + at % 128), (1, tiny))[0]

    dec_b = jnp.pad(small[:, :cols].astype(BF16), ((0, piece - dec_rows), (0, 0)))
    mine = jnp.concatenate([mine, dec_b], axis=1)
    over_t = lax.all_to_all(
        jnp.broadcast_to(mine[None], (NT, *mine.shape)), TP, 0, 0, tiled=True
    )
    got = ring_send(ring_add(chunk, 1, got))
    red = chunk(0, 1).astype(F32) + got[0].astype(F32) + got[1].astype(F32)
    red = red.astype(BF16)
    whole_rows = over_t[:, :, :out_w].reshape(rows, out_w)
    grad_input = whole_rows[:, :width]
    output = (tokens.astype(F32) + dot(whole_rows[:, width:], decoder)).astype(BF16)
    grad_decoder = over_t[:, :dec_rows, out_w:].astype(F32)
    grad_decoder = grad_decoder.transpose(1, 0, 2).reshape(dec_rows, width)

    red = red.reshape(YH, CORES * fine, 4 * own)
    away = lax.dynamic_index_in_dim(red, 1 - yh, 0, keepdims=False)
    here = lax.dynamic_index_in_dim(red, yh, 0, keepdims=False)
    both = here.astype(F32) + lax.ppermute(away, "yh", SWAP).astype(F32)
    both = both.astype(BF16).reshape(CORES, fine, 4 * own)
    here = lax.dynamic_index_in_dim(both, c, 0, keepdims=False)
    away = lax.dynamic_index_in_dim(both, 1 - c, 0, keepdims=False)
    away = lax.ppermute(away, "c", SWAP)
    low = jnp.where(c == 0, here, away).astype(F32)
    high = jnp.where(c == 0, away, here).astype(F32)
    grads = [
        jnp.concatenate(
            [low[:, i * own : (i + 1) * own], high[:, i * own : (i + 1) * own]], axis=1
        )
        for i in range(4)
    ]
    return (
        output,
        grad_input,
        grad_gain,
        grads[0],
        grads[1],
        grads[2],
        grads[3].T,
        grad_encoder,
        grad_decoder,
    )


def solution(mesh):
    devices = np.asarray(mesh.devices).reshape(YH, Z, CORES, YL, X)
    fine = Mesh(devices, ("yh", "z", "c", "yl", "x"))
    dp = ("yh", "z", "c")
    every = (*dp, *TP)
    return jax.shard_map(
        on_device,
        mesh=fine,
        in_specs=(
            P(dp, None),
            P(),
            P(None, TP),
            P(None, TP),
            P(None, TP),
            P(TP, None),
            P(),
            P(),
            P(dp, None),
        ),
        out_specs=(
            P(dp, None),
            P(dp, None),
            P(every),
            P(dp, TP),
            P(dp, TP),
            P(dp, TP),
            P(TP, dp),
            P(every, None),
            P(dp, None),
        ),
        check_vma=False,
    )
```

```python
import functools

import jax
import jax.numpy as jnp
import numpy as np
from jax import lax
from jax.experimental import pallas as pl
from jax.experimental.pallas import tpu as pltpu
from jax.sharding import Mesh
from jax.sharding import PartitionSpec as P

DK = 128
SEQ = 256
YH, Z, CORES, YL, X = 2, 8, 2, 2, 4
NT = YL * X
TP = ("yl", "x")
F32 = jnp.float32
BF16 = jnp.bfloat16
SWAP = [(0, 1), (1, 0)]


def dot(a, b, ca=1, cb=0):
    return lax.dot_general(a, b, (((ca,), (cb,)), ((), ())), preferred_element_type=F32)


def block_kernel(
    core_ref,
    gain,
    tok_own_h,
    tok_oth_h,
    wq_h,
    cot_own_h,
    cot_oth_h,
    dec_h,
    wo_h,
    enc_h,
    wk_h,
    wv_h,
    buf_h,
    keep,
    send,
    first_up,
    first_down,
    tok,
    cot,
    wq,
    wk,
    wv,
    wo,
    enc,
    dec,
    norm_s,
    norm_t,
    dcode_s,
    q_s,
    k_s,
    v_s,
    dctx_s,
    ctx_s,
    dq_s,
    dk_s,
    dv_s,
    code_s,
    stage,
    rms_s,
    enc_s,
    small_s,
    in_sem,
    out_sem,
):
    width, own = wq.shape
    heads = own // DK
    code = enc.shape[1]
    part = width // (YH * Z)
    core = core_ref[0]
    far = lax.rem(core_ref[1] + Z // 2, Z)
    mine = pl.ds(pl.multiple_of(core * own, own), own)
    pairs = (
        (tok_own_h, tok.at[pl.ds(0, SEQ)]),
        (tok_oth_h, tok.at[pl.ds(SEQ, SEQ)]),
        (wq_h.at[:, mine], wq),
        (wk_h.at[:, mine], wk),
        (wv_h.at[:, mine], wv),
        (cot_own_h, cot.at[pl.ds(0, SEQ)]),
        (cot_oth_h, cot.at[pl.ds(SEQ, SEQ)]),
        (dec_h, dec),
        (wo_h.at[mine, :], wo),
        (enc_h, enc),
    )
    copies = [pltpu.make_async_copy(a, b, in_sem.at[i]) for i, (a, b) in enumerate(pairs)]
    for copy in copies:
        copy.start()

    for s in range(2):
        at = slice(s * SEQ, (s + 1) * SEQ)
        copies[s].wait()
        x = tok[at, :].astype(F32)
        rms = lax.rsqrt(jnp.mean(x * x, axis=-1, keepdims=True) + 1e-6)
        rms_s[at, :] = jnp.broadcast_to(rms, (SEQ, 128))
        norm_s[at, :] = (x * rms * gain[...]).astype(BF16)
    normed = norm_s[...]
    copies[2].wait()
    q_s[...] = dot(normed, wq[...]).astype(BF16)
    norm_t[...] = normed.T
    copies[3].wait()
    k_s[...] = dot(normed, wk[...]).astype(BF16)
    copies[4].wait()
    v_s[...] = dot(normed, wv[...]).astype(BF16)
    for copy in copies[5:]:
        copy.wait()
    dcode_s[...] = dot(cot[...], dec[...], 1, 1).astype(BF16)
    w2 = dot(wo[...], enc[...]).astype(BF16)
    dctx_s[...] = dot(dcode_s[...], w2, 1, 1).astype(BF16)
    scale = DK**-0.5
    row = lax.broadcasted_iota(jnp.int32, (SEQ, SEQ), 0)
    col = lax.broadcasted_iota(jnp.int32, (SEQ, SEQ), 1)
    causal = row <= col
    log2 = scale * 1.4426950408889634
    for s in range(2):
        for h in range(heads):
            at = (slice(s * SEQ, (s + 1) * SEQ), slice(h * DK, (h + 1) * DK))
            q, k, v, dctx = q_s[at], k_s[at], v_s[at], dctx_s[at]
            scores = jnp.where(causal, dot(k, q, 1, 1), -1e30)
            top = jnp.max(scores, axis=0, keepdims=True)
            expo = jnp.exp2((scores - top) * log2)
            probs = expo * (1.0 / jnp.sum(expo, axis=0, keepdims=True))
            low = probs.astype(BF16)
            ctx_s[at] = dot(low, v, 0, 0).astype(BF16)
            dprobs = dot(v, dctx, 1, 1)
            dv_s[at] = dot(low, dctx).astype(BF16)
            delta = jnp.sum(dprobs * probs, axis=0, keepdims=True)
            ds = (probs * (dprobs - delta) * scale).astype(BF16)
            dq_s[at] = dot(ds, k, 0, 0).astype(BF16)
            dk_s[at] = dot(ds, q).astype(BF16)

    def put(i, g):
        lanes = slice(i * own, (i + 1) * own)
        for z in range(Z):
            for y in range(YH):
                at = (y * Z + z) * part
                stage[z, y * part : (y + 1) * part, lanes] = g[at : at + part, :].astype(BF16)
        there = buf_h.at[:, :, pl.ds(i * own, own)]
        copy = pltpu.make_async_copy(stage.at[:, :, pl.ds(i * own, own)], there, out_sem.at[i])
        copy.start()
        return copy

    g = dot(ctx_s[...], dcode_s[...], 0, 0).astype(BF16)
    out = [put(3, dot(enc[...], g, 1, 1))]
    out.append(put(2, dot(norm_t[...], dv_s[...])))
    out.append(put(0, dot(norm_t[...], dq_s[...])))
    out.append(put(1, dot(norm_t[...], dk_s[...])))
    for i in range(2):
        half = YH * part // 2
        (first_up, first_down)[i][...] = stage[far, i * half : (i + 1) * half, :]
    piece = SEQ // NT
    code_s[...] = dot(ctx_s[...], w2).astype(BF16)
    gain_p = jnp.zeros((1, width), F32)
    for s in range(2):
        at = slice(s * SEQ, (s + 1) * SEQ)
        dn = dot(dq_s[at, :], wq[...], 1, 1)
        dn = dn + dot(dk_s[at, :], wk[...], 1, 1)
        dn = dn + dot(dv_s[at, :], wv[...], 1, 1)
        unit = tok[at, :].astype(F32) * rms_s[at, 0:1]
        gain_p = gain_p + jnp.sum(dn * unit, axis=0, keepdims=True)
        low = dn.astype(BF16)
        for t in range(NT):
            here = slice(t * piece, (t + 1) * piece)
            there = slice(s * SEQ + t * piece, s * SEQ + (t + 1) * piece)
            ref = (keep, send)[s]
            ref[t, :, 0:width] = low[here, :]
            ref[t, :, width : width + code] = code_s[there, :]
    enc_s[...] = dot(wo[...], g, 0, 0)
    dec_p = dot(code_s[...], cot[...], 0, 0).astype(BF16)
    n_yz = YH * Z
    fine = part // CORES
    tiny = fine // NT
    rows = code // n_yz // CORES
    cols = width // NT
    blocks = n_yz * rows // piece
    each = piece // rows
    base = width + code
    for cc in range(CORES):
        small = small_s.at[jnp.where(core == cc, 0, 1)]
        for t in range(NT):
            for j in range(blocks):
                dec_at = j * 2 * cols
                dec_b, enc_b = [], []
                for yz in range(j * each, (j + 1) * each):
                    r = (yz * CORES + cc) * rows
                    dec_b.append(dec_p[r : r + rows, t * cols : (t + 1) * cols])
                    e = (yz * CORES + cc) * fine + t * tiny
                    enc_b.append(enc_s[e : e + tiny, 0:cols])
                    enc_b.append(enc_s[e : e + tiny, cols : 2 * cols])
                small[t, :, dec_at : dec_at + cols] = jnp.concatenate(dec_b, axis=0)
                enc_v = jnp.concatenate(enc_b, axis=0).astype(BF16)
                small[t, :, dec_at + cols : dec_at + 2 * cols] = enc_v
    gain_v = jnp.concatenate(
        [gain_p[:, i * 128 : (i + 1) * 128] for i in range(width // 128)]
        + [jnp.zeros((piece - width // 128, 128), F32)],
        axis=0,
    ).astype(BF16)
    end = base + blocks * 2 * cols
    for s, ref in enumerate((keep, send)):
        ref[:, :, base:end] = small_s[s]
        for t in range(NT):
            ref[t, :, end:] = gain_v
    for copy in out:
        copy.wait()


def run_block(core, gain, *args):
    tokens, wq, enc = args[0], args[2], args[7]
    width, own = wq.shape[0], wq.shape[1] // CORES
    code = enc.shape[1]
    part = width // (YH * Z)
    sds = jax.ShapeDtypeStruct
    piece = SEQ // NT
    lanes = width + code + width + 128
    outs = (
        sds((Z, YH * part, 4 * own), BF16),
        sds((NT, piece, lanes), BF16),
        sds((NT, piece, lanes), BF16),
        sds((YH * part // 2, 4 * own), BF16),
        sds((YH * part // 2, 4 * own), BF16),
    )
    vmem = pl.BlockSpec(memory_space=pltpu.VMEM)
    hbm = pl.BlockSpec(memory_space=pl.ANY)
    two = 2 * SEQ
    shapes = (
        (two, width),
        (two, width),
        (width, own),
        (width, own),
        (width, own),
        (own, width),
        (width, code),
        (code, width),
        (two, width),
        (width, two),
        (two, code),
        *(((two, own),) * 8),
        (two, code),
        (Z, YH * part, 4 * own),
    )
    return pl.pallas_call(
        block_kernel,
        in_specs=[pl.BlockSpec(memory_space=pltpu.SMEM), vmem, *([hbm] * len(args))],
        out_specs=[hbm, vmem, vmem, vmem, vmem],
        out_shape=outs,
        scratch_shapes=[
            *(pltpu.VMEM(shape, BF16) for shape in shapes),
            pltpu.VMEM((two, 128), F32),
            pltpu.VMEM((width, code), F32),
            pltpu.VMEM((2, NT, piece, width), BF16),
            pltpu.SemaphoreType.DMA((10,)),
            pltpu.SemaphoreType.DMA((4,)),
        ],
        compiler_params=pltpu.CompilerParams(vmem_limit_bytes=56 * 1024 * 1024),
        cost_estimate=pl.CostEstimate(
            flops=7_500_000_000, bytes_accessed=14_000_000, transcendentals=600_000
        ),
    )(core, gain, *args)


def ring_chunk(buf, z, c, k, sign):
    turn = k * sign * (1 - 2 * c)
    return lax.dynamic_index_in_dim(buf, lax.rem(z + turn + Z, Z), 0, keepdims=False)


def ring_send(a, sign):
    pairs = [
        (at * CORES + core, (at + sign * (1 - 2 * core)) % Z * CORES + core)
        for at in range(Z)
        for core in range(CORES)
    ]
    return lax.ppermute(a, ("z", "c"), pairs)


def ring_add(local, a, sign):
    half = local.shape[0] // 2
    if a.shape[0] == local.shape[0]:
        return (local.astype(F32) + a.astype(F32)).astype(BF16)
    rows = slice(0, half) if sign == 1 else slice(half, 2 * half)
    added = (local[rows].astype(F32) + a.astype(F32)).astype(BF16)
    parts = [added, local[half:]] if sign == 1 else [local[:half], added]
    return jnp.concatenate(parts, axis=0)


def tie(*arrays):
    return lax.optimization_barrier(arrays)


def spread_kernel(core_ref, here, away, *outs):
    own = outs[0].shape[1] // CORES
    core = core_ref[0]
    for ref, at in ((here, core), (away, 1 - core)):
        lanes = pl.ds(pl.multiple_of(at * own, own), own)
        for i, out in enumerate(outs):
            out[:, lanes] = ref[:, i * own : (i + 1) * own].astype(F32)


def spread(core, here, away):
    rows, own = here.shape[0], here.shape[1] // 4
    vmem = pl.BlockSpec(memory_space=pltpu.VMEM)
    return pl.pallas_call(
        spread_kernel,
        in_specs=[pl.BlockSpec(memory_space=pltpu.SMEM), vmem, vmem],
        out_specs=[vmem] * 4,
        out_shape=[jax.ShapeDtypeStruct((rows, CORES * own), F32)] * 4,
        compiler_params=pltpu.CompilerParams(vmem_limit_bytes=16 * 1024 * 1024),
    )(core, here, away)


def on_device(tokens, gain, w_query, w_key, w_value, w_output, encoder, decoder, cotangent):
    rows, width = tokens.shape
    own = w_query.shape[1] // CORES
    code_w = encoder.shape[1]
    yh, z, c = lax.axis_index("yh"), lax.axis_index("z"), lax.axis_index("c")
    t = lax.axis_index("yl") * X + lax.axis_index("x")
    n_dp = YH * Z * CORES
    fine = width // n_dp
    tiny = fine // NT
    core = jnp.stack([c, z]).astype(jnp.int32)

    tok_oth = lax.ppermute(tokens, "c", SWAP)
    cot_oth = lax.ppermute(cotangent, "c", SWAP)
    buf, keep, send, first_up, first_down = run_block(
        core,
        gain.reshape(1, width),
        tokens,
        tok_oth,
        w_query,
        cotangent,
        cot_oth,
        decoder,
        w_output,
        encoder,
        w_key,
        w_value,
    )
    chunk = functools.partial(ring_chunk, buf, z, c)
    up = ring_send(first_up, 1)
    down = ring_send(first_down, -1)
    both = (keep.astype(F32) + lax.ppermute(send, "c", SWAP).astype(F32)).astype(BF16)
    up, both = tie(up, both)
    up = ring_add(chunk(3, 1), up, 1)
    up, down, both = tie(up, down, both)
    over_t = lax.all_to_all(both, TP, 0, 0, tiled=True)
    up = ring_send(up, 1)
    down = ring_send(ring_add(chunk(3, -1), down, -1), -1)
    up = ring_add(chunk(2, 1), up, 1)
    up, down = tie(up, down)
    up = ring_send(up, 1)
    total = jnp.sum(over_t.astype(F32), axis=0)
    piece = rows // NT
    out_w = width + code_w
    cols = width // NT
    dec_rows = code_w // n_dp
    small = total[:, out_w : out_w + width]
    small = jnp.concatenate(
        [small[:, i * 2 * cols : (i + 1) * 2 * cols] for i in range(width // (2 * cols))], axis=0
    ).reshape(YH * Z, dec_rows, 2 * cols)
    gain_v = total[: width // 128, out_w + width :]
    small = jnp.concatenate(
        [small, jnp.broadcast_to(gain_v[None], (YH * Z, *gain_v.shape))], axis=2
    ).astype(BF16)
    small, down = tie(small, down)
    small = lax.all_to_all(small, ("yh", "z"), 0, 0, tiled=True)
    down = ring_send(ring_add(chunk(2, -1), down, -1), -1)
    up = ring_add(chunk(1, 1), up, 1)
    up, down = tie(up, down)
    up = ring_send(up, 1)

    dnormed = total[:, :width]
    x = lax.dynamic_slice_in_dim(tokens, t * piece, piece, 0).astype(F32)
    cot = lax.dynamic_slice_in_dim(cotangent, t * piece, piece, 0).astype(F32)
    rms = lax.rsqrt(jnp.mean(x * x, axis=-1, keepdims=True) + 1e-6)
    unit = x * rms
    dunit = dnormed * gain
    inner = jnp.sum(dunit * unit, axis=-1, keepdims=True) / width
    grad_rows = cot + rms * (dunit - unit * inner)
    mine = jnp.concatenate([grad_rows, total[:, width:out_w]], axis=1).astype(BF16)

    small = jnp.sum(small.astype(F32), axis=0)
    enc_v = small[:, cols : 2 * cols]
    grad_encoder = jnp.concatenate([enc_v[:tiny], enc_v[tiny:]], axis=1)
    at = (((yh * Z + z) * CORES + c) * NT + t) * tiny
    grad_gain = lax.dynamic_slice(small, (at // 128, 2 * cols + at % 128), (1, tiny))[0]

    dec_b = jnp.pad(small[:, :cols].astype(BF16), ((0, piece - dec_rows), (0, 0)))
    mine = jnp.concatenate([mine, dec_b], axis=1)
    mine, down = tie(mine, down)
    over_t = lax.all_to_all(
        jnp.broadcast_to(mine[None], (NT, *mine.shape)), TP, 0, 0, tiled=True
    )
    down = ring_send(ring_add(chunk(1, -1), down, -1), -1)
    red = (chunk(0, 1).astype(F32) + up.astype(F32) + down.astype(F32)).astype(BF16)
    whole_rows = over_t[:, :, :out_w].reshape(rows, out_w)
    grad_input = whole_rows[:, :width]
    output = (tokens.astype(F32) + dot(whole_rows[:, width:], decoder)).astype(BF16)
    grad_decoder = over_t[:, :dec_rows, out_w:].astype(F32)
    grad_decoder = grad_decoder.transpose(1, 0, 2).reshape(dec_rows, width)

    red = red.reshape(YH, CORES * fine, 4 * own)
    away = lax.dynamic_index_in_dim(red, 1 - yh, 0, keepdims=False)
    here = lax.dynamic_index_in_dim(red, yh, 0, keepdims=False)
    both = here.astype(F32) + lax.ppermute(away, "yh", SWAP).astype(F32)
    both = both.astype(BF16).reshape(CORES, fine, 4 * own)
    here = lax.dynamic_index_in_dim(both, c, 0, keepdims=False)
    away = lax.dynamic_index_in_dim(both, 1 - c, 0, keepdims=False)
    away = lax.ppermute(away, "c", SWAP)
    grads = spread(core, here, away)

    return (
        output,
        grad_input,
        grad_gain,
        grads[0],
        grads[1],
        grads[2],
        grads[3].T,
        grad_encoder,
        grad_decoder,
    )


def solution(mesh):
    devices = np.asarray(mesh.devices).reshape(YH, Z, CORES, YL, X)
    fine = Mesh(devices, ("yh", "z", "c", "yl", "x"))
    dp = ("yh", "z", "c")
    every = (*dp, *TP)
    return jax.shard_map(
        on_device,
        mesh=fine,
        in_specs=(
            P(dp, None),
            P(),
            P(None, TP),
            P(None, TP),
            P(None, TP),
            P(TP, None),
            P(),
            P(),
            P(dp, None),
        ),
        out_specs=(
            P(dp, None),
            P(dp, None),
            P(every),
            P(dp, TP),
            P(dp, TP),
            P(dp, TP),
            P(TP, dp),
            P(every, None),
            P(dp, None),
        ),
        check_vma=False,
    )
```

```python
import functools

import jax
import jax.numpy as jnp
import numpy as np
from jax import lax
from jax.experimental import pallas as pl
from jax.experimental.pallas import tpu as pltpu
from jax.sharding import Mesh
from jax.sharding import PartitionSpec as P

DK = 128
SEQ = 256
YH, Z, CORES, YL, X = 2, 8, 2, 2, 4
NT = YL * X
TP = ("yl", "x")
F32 = jnp.float32
BF16 = jnp.bfloat16
SWAP = [(0, 1), (1, 0)]


def dot(a, b, ca=1, cb=0):
    return lax.dot_general(a, b, (((ca,), (cb,)), ((), ())), preferred_element_type=F32)


def block_kernel(
    core_ref,
    gain,
    tok_own_h,
    tok_oth_h,
    wq_h,
    cot_own_h,
    cot_oth_h,
    dec_h,
    wo_h,
    enc_h,
    wk_h,
    wv_h,
    buf_h,
    keep,
    send,
    first_up,
    first_down,
    tok,
    cot,
    wq,
    wk,
    wv,
    wo,
    enc,
    dec,
    norm_s,
    norm_t,
    dcode_s,
    q_s,
    k_s,
    v_s,
    dctx_s,
    ctx_s,
    dq_s,
    dk_s,
    dv_s,
    code_s,
    stage,
    rms_s,
    enc_s,
    small_s,
    in_sem,
    out_sem,
):
    width, own = wq.shape
    heads = own // DK
    code = enc.shape[1]
    part = width // (YH * Z)
    core = core_ref[0]
    far = lax.rem(core_ref[1] + Z // 2, Z)
    mine = pl.ds(pl.multiple_of(core * own, own), own)
    pairs = (
        (tok_own_h, tok.at[pl.ds(0, SEQ)]),
        (tok_oth_h, tok.at[pl.ds(SEQ, SEQ)]),
        (wq_h.at[:, mine], wq),
        (wk_h.at[:, mine], wk),
        (wv_h.at[:, mine], wv),
        (cot_own_h, cot.at[pl.ds(0, SEQ)]),
        (cot_oth_h, cot.at[pl.ds(SEQ, SEQ)]),
        (dec_h, dec),
        (wo_h.at[mine, :], wo),
        (enc_h, enc),
    )
    copies = [pltpu.make_async_copy(a, b, in_sem.at[i]) for i, (a, b) in enumerate(pairs)]
    for copy in copies:
        copy.start()

    for s in range(2):
        at = slice(s * SEQ, (s + 1) * SEQ)
        copies[s].wait()
        x = tok[at, :].astype(F32)
        rms = lax.rsqrt(jnp.mean(x * x, axis=-1, keepdims=True) + 1e-6)
        rms_s[at, :] = jnp.broadcast_to(rms, (SEQ, 128))
        norm_s[at, :] = (x * rms * gain[...]).astype(BF16)
    normed = norm_s[...]
    copies[2].wait()
    q_s[...] = dot(normed, wq[...]).astype(BF16)
    norm_t[...] = normed.T
    copies[3].wait()
    k_s[...] = dot(normed, wk[...]).astype(BF16)
    copies[4].wait()
    v_s[...] = dot(normed, wv[...]).astype(BF16)
    for copy in copies[5:]:
        copy.wait()
    dcode_s[...] = dot(cot[...], dec[...], 1, 1).astype(BF16)
    w2 = dot(wo[...], enc[...]).astype(BF16)
    dctx_s[...] = dot(dcode_s[...], w2, 1, 1).astype(BF16)
    scale = DK**-0.5
    row = lax.broadcasted_iota(jnp.int32, (SEQ, SEQ), 0)
    col = lax.broadcasted_iota(jnp.int32, (SEQ, SEQ), 1)
    causal = row <= col
    log2 = scale * 1.4426950408889634
    for s in range(2):
        for h in range(heads):
            at = (slice(s * SEQ, (s + 1) * SEQ), slice(h * DK, (h + 1) * DK))
            q, k, v, dctx = q_s[at], k_s[at], v_s[at], dctx_s[at]
            scores = jnp.where(causal, dot(k, q, 1, 1), -1e30)
            top = jnp.max(scores, axis=0, keepdims=True)
            expo = jnp.exp2((scores - top) * log2)
            probs = expo * (1.0 / jnp.sum(expo, axis=0, keepdims=True))
            low = probs.astype(BF16)
            ctx_s[at] = dot(low, v, 0, 0).astype(BF16)
            dprobs = dot(v, dctx, 1, 1)
            dv_s[at] = dot(low, dctx).astype(BF16)
            delta = jnp.sum(dprobs * probs, axis=0, keepdims=True)
            ds = (probs * (dprobs - delta) * scale).astype(BF16)
            dq_s[at] = dot(ds, k, 0, 0).astype(BF16)
            dk_s[at] = dot(ds, q).astype(BF16)

    def put(i, g):
        lanes = slice(i * own, (i + 1) * own)
        for z in range(Z):
            for y in range(YH):
                at = (y * Z + z) * part
                stage[z, y * part : (y + 1) * part, lanes] = g[at : at + part, :].astype(BF16)
        there = buf_h.at[:, :, pl.ds(i * own, own)]
        copy = pltpu.make_async_copy(stage.at[:, :, pl.ds(i * own, own)], there, out_sem.at[i])
        copy.start()
        return copy

    g = dot(ctx_s[...], dcode_s[...], 0, 0).astype(BF16)
    out = [put(3, dot(enc[...], g, 1, 1))]
    out.append(put(2, dot(norm_t[...], dv_s[...])))
    out.append(put(0, dot(norm_t[...], dq_s[...])))
    out.append(put(1, dot(norm_t[...], dk_s[...])))
    for i in range(2):
        half = YH * part // 2
        (first_up, first_down)[i][...] = stage[far, i * half : (i + 1) * half, :]
    piece = SEQ // NT
    code_s[...] = dot(ctx_s[...], w2).astype(BF16)
    gain_p = jnp.zeros((1, width), F32)
    for s in range(2):
        at = slice(s * SEQ, (s + 1) * SEQ)
        dn = dot(dq_s[at, :], wq[...], 1, 1)
        dn = dn + dot(dk_s[at, :], wk[...], 1, 1)
        dn = dn + dot(dv_s[at, :], wv[...], 1, 1)
        unit = tok[at, :].astype(F32) * rms_s[at, 0:1]
        gain_p = gain_p + jnp.sum(dn * unit, axis=0, keepdims=True)
        low = dn.astype(BF16)
        for t in range(NT):
            here = slice(t * piece, (t + 1) * piece)
            there = slice(s * SEQ + t * piece, s * SEQ + (t + 1) * piece)
            ref = (keep, send)[s]
            ref[t, :, 0:width] = low[here, :]
            ref[t, :, width : width + code] = code_s[there, :]
    enc_s[...] = dot(wo[...], g, 0, 0)
    dec_p = dot(code_s[...], cot[...], 0, 0).astype(BF16)
    n_yz = YH * Z
    fine = part // CORES
    tiny = fine // NT
    rows = code // n_yz // CORES
    cols = width // NT
    blocks = n_yz * rows // piece
    each = piece // rows
    base = width + code
    for cc in range(CORES):
        small = small_s.at[jnp.where(core == cc, 0, 1)]
        for t in range(NT):
            for j in range(blocks):
                dec_at = j * 2 * cols
                dec_b, enc_b = [], []
                for yz in range(j * each, (j + 1) * each):
                    r = (yz * CORES + cc) * rows
                    dec_b.append(dec_p[r : r + rows, t * cols : (t + 1) * cols])
                    e = (yz * CORES + cc) * fine + t * tiny
                    enc_b.append(enc_s[e : e + tiny, 0:cols])
                    enc_b.append(enc_s[e : e + tiny, cols : 2 * cols])
                small[t, :, dec_at : dec_at + cols] = jnp.concatenate(dec_b, axis=0)
                enc_v = jnp.concatenate(enc_b, axis=0).astype(BF16)
                small[t, :, dec_at + cols : dec_at + 2 * cols] = enc_v
    gain_v = jnp.concatenate(
        [gain_p[:, i * 128 : (i + 1) * 128] for i in range(width // 128)]
        + [jnp.zeros((piece - width // 128, 128), F32)],
        axis=0,
    ).astype(BF16)
    end = base + blocks * 2 * cols
    for s, ref in enumerate((keep, send)):
        ref[:, :, base:end] = small_s[s]
        for t in range(NT):
            ref[t, :, end:] = gain_v
    for copy in out:
        copy.wait()


def run_block(core, gain, *args):
    tokens, wq, enc = args[0], args[2], args[7]
    width, own = wq.shape[0], wq.shape[1] // CORES
    code = enc.shape[1]
    part = width // (YH * Z)
    sds = jax.ShapeDtypeStruct
    piece = SEQ // NT
    lanes = width + code + width + 128
    outs = (
        sds((Z, YH * part, 4 * own), BF16),
        sds((NT, piece, lanes), BF16),
        sds((NT, piece, lanes), BF16),
        sds((YH * part // 2, 4 * own), BF16),
        sds((YH * part // 2, 4 * own), BF16),
    )
    vmem = pl.BlockSpec(memory_space=pltpu.VMEM)
    hbm = pl.BlockSpec(memory_space=pl.ANY)
    two = 2 * SEQ
    shapes = (
        (two, width),
        (two, width),
        (width, own),
        (width, own),
        (width, own),
        (own, width),
        (width, code),
        (code, width),
        (two, width),
        (width, two),
        (two, code),
        *(((two, own),) * 8),
        (two, code),
        (Z, YH * part, 4 * own),
    )
    return pl.pallas_call(
        block_kernel,
        in_specs=[pl.BlockSpec(memory_space=pltpu.SMEM), vmem, *([hbm] * len(args))],
        out_specs=[hbm, vmem, vmem, vmem, vmem],
        out_shape=outs,
        scratch_shapes=[
            *(pltpu.VMEM(shape, BF16) for shape in shapes),
            pltpu.VMEM((two, 128), F32),
            pltpu.VMEM((width, code), F32),
            pltpu.VMEM((2, NT, piece, width), BF16),
            pltpu.SemaphoreType.DMA((10,)),
            pltpu.SemaphoreType.DMA((4,)),
        ],
        compiler_params=pltpu.CompilerParams(vmem_limit_bytes=56 * 1024 * 1024),
        cost_estimate=pl.CostEstimate(
            flops=7_500_000_000, bytes_accessed=14_000_000, transcendentals=600_000
        ),
    )(core, gain, *args)


def ring_chunk(buf, z, c, k, sign):
    turn = k * sign * (1 - 2 * c)
    return lax.dynamic_index_in_dim(buf, lax.rem(z + turn + Z, Z), 0, keepdims=False)


def ring_send(a, sign):
    pairs = [
        (at * CORES + core, (at + sign * (1 - 2 * core)) % Z * CORES + core)
        for at in range(Z)
        for core in range(CORES)
    ]
    return lax.ppermute(a, ("z", "c"), pairs)


def ring_add(local, a, sign):
    half = local.shape[0] // 2
    if a.shape[0] == local.shape[0]:
        return (local.astype(F32) + a.astype(F32)).astype(BF16)
    rows = slice(0, half) if sign == 1 else slice(half, 2 * half)
    added = (local[rows].astype(F32) + a.astype(F32)).astype(BF16)
    parts = [added, local[half:]] if sign == 1 else [local[:half], added]
    return jnp.concatenate(parts, axis=0)


def tie(*arrays):
    return lax.optimization_barrier(arrays)


def spread_kernel(core_ref, here, away, *outs):
    own = outs[0].shape[1] // CORES
    core = core_ref[0]
    for ref, at in ((here, core), (away, 1 - core)):
        lanes = pl.ds(pl.multiple_of(at * own, own), own)
        for i, out in enumerate(outs):
            out[:, lanes] = ref[:, i * own : (i + 1) * own].astype(F32)


def spread(core, here, away):
    rows, own = here.shape[0], here.shape[1] // 4
    vmem = pl.BlockSpec(memory_space=pltpu.VMEM)
    return pl.pallas_call(
        spread_kernel,
        in_specs=[pl.BlockSpec(memory_space=pltpu.SMEM), vmem, vmem],
        out_specs=[vmem] * 4,
        out_shape=[jax.ShapeDtypeStruct((rows, CORES * own), F32)] * 4,
        compiler_params=pltpu.CompilerParams(vmem_limit_bytes=16 * 1024 * 1024),
    )(core, here, away)


def on_device(tokens, gain, w_query, w_key, w_value, w_output, encoder, decoder, cotangent):
    rows, width = tokens.shape
    own = w_query.shape[1] // CORES
    code_w = encoder.shape[1]
    yh, z, c = lax.axis_index("yh"), lax.axis_index("z"), lax.axis_index("c")
    t = lax.axis_index("yl") * X + lax.axis_index("x")
    n_dp = YH * Z * CORES
    fine = width // n_dp
    tiny = fine // NT
    core = jnp.stack([c, z]).astype(jnp.int32)

    tok_oth = lax.ppermute(tokens, "c", SWAP)
    cot_oth = lax.ppermute(cotangent, "c", SWAP)
    buf, keep, send, first_up, first_down = run_block(
        core,
        gain.reshape(1, width),
        tokens,
        tok_oth,
        w_query,
        cotangent,
        cot_oth,
        decoder,
        w_output,
        encoder,
        w_key,
        w_value,
    )
    chunk = functools.partial(ring_chunk, buf, z, c)
    up = ring_send(first_up, 1)
    down = ring_send(first_down, -1)
    both = (keep.astype(F32) + lax.ppermute(send, "c", SWAP).astype(F32)).astype(BF16)
    up, _ = tie(up, both)
    up = ring_add(chunk(3, 1), up, 1)
    up, down = tie(up, down)
    over_t = lax.all_to_all(both, TP, 0, 0, tiled=True)
    up = ring_send(up, 1)
    down = ring_send(ring_add(chunk(3, -1), down, -1), -1)
    total = jnp.sum(over_t.astype(F32), axis=0)
    piece = rows // NT
    out_w = width + code_w
    cols = width // NT
    dec_rows = code_w // n_dp
    small = total[:, out_w : out_w + width]
    small = jnp.concatenate(
        [small[:, i * 2 * cols : (i + 1) * 2 * cols] for i in range(width // (2 * cols))], axis=0
    ).reshape(YH * Z, dec_rows, 2 * cols)
    gain_v = total[: width // 128, out_w + width :]
    small = jnp.concatenate(
        [small, jnp.broadcast_to(gain_v[None], (YH * Z, *gain_v.shape))], axis=2
    ).astype(BF16)
    small, up = tie(small, up)
    small = lax.all_to_all(small, ("yh", "z"), 0, 0, tiled=True)
    up = ring_add(chunk(2, 1), up, 1)
    up, down = tie(up, down)
    up = ring_send(up, 1)
    down = ring_send(ring_add(chunk(2, -1), down, -1), -1)
    up = ring_add(chunk(1, 1), up, 1)
    up, down = tie(up, down)
    up = ring_send(up, 1)

    dnormed = total[:, :width]
    x = lax.dynamic_slice_in_dim(tokens, t * piece, piece, 0).astype(F32)
    cot = lax.dynamic_slice_in_dim(cotangent, t * piece, piece, 0).astype(F32)
    rms = lax.rsqrt(jnp.mean(x * x, axis=-1, keepdims=True) + 1e-6)
    unit = x * rms
    dunit = dnormed * gain
    inner = jnp.sum(dunit * unit, axis=-1, keepdims=True) / width
    grad_rows = cot + rms * (dunit - unit * inner)
    mine = jnp.concatenate([grad_rows, total[:, width:out_w]], axis=1).astype(BF16)

    small = jnp.sum(small.astype(F32), axis=0)
    enc_v = small[:, cols : 2 * cols]
    grad_encoder = jnp.concatenate([enc_v[:tiny], enc_v[tiny:]], axis=1)
    at = (((yh * Z + z) * CORES + c) * NT + t) * tiny
    grad_gain = lax.dynamic_slice(small, (at // 128, 2 * cols + at % 128), (1, tiny))[0]

    dec_b = jnp.pad(small[:, :cols].astype(BF16), ((0, piece - dec_rows), (0, 0)))
    mine = jnp.concatenate([mine, dec_b], axis=1)
    mine, down = tie(mine, down)
    over_t = lax.all_to_all(
        jnp.broadcast_to(mine[None], (NT, *mine.shape)), TP, 0, 0, tiled=True
    )
    down = ring_send(ring_add(chunk(1, -1), down, -1), -1)
    red = (chunk(0, 1).astype(F32) + up.astype(F32) + down.astype(F32)).astype(BF16)
    whole_rows = over_t[:, :, :out_w].reshape(rows, out_w)
    grad_input = whole_rows[:, :width]
    output = (tokens.astype(F32) + dot(whole_rows[:, width:], decoder)).astype(BF16)
    grad_decoder = over_t[:, :dec_rows, out_w:].astype(F32)
    grad_decoder = grad_decoder.transpose(1, 0, 2).reshape(dec_rows, width)

    red = red.reshape(YH, CORES * fine, 4 * own)
    away = lax.dynamic_index_in_dim(red, 1 - yh, 0, keepdims=False)
    here = lax.dynamic_index_in_dim(red, yh, 0, keepdims=False)
    both = here.astype(F32) + lax.ppermute(away, "yh", SWAP).astype(F32)
    both = both.astype(BF16).reshape(CORES, fine, 4 * own)
    here = lax.dynamic_index_in_dim(both, c, 0, keepdims=False)
    away = lax.dynamic_index_in_dim(both, 1 - c, 0, keepdims=False)
    away = lax.ppermute(away, "c", SWAP)
    grads = spread(core, here, away)

    return (
        output,
        grad_input,
        grad_gain,
        grads[0],
        grads[1],
        grads[2],
        grads[3].T,
        grad_encoder,
        grad_decoder,
    )


def solution(mesh):
    devices = np.asarray(mesh.devices).reshape(YH, Z, CORES, YL, X)
    fine = Mesh(devices, ("yh", "z", "c", "yl", "x"))
    dp = ("yh", "z", "c")
    every = (*dp, *TP)
    return jax.shard_map(
        on_device,
        mesh=fine,
        in_specs=(
            P(dp, None),
            P(),
            P(None, TP),
            P(None, TP),
            P(None, TP),
            P(TP, None),
            P(),
            P(),
            P(dp, None),
        ),
        out_specs=(
            P(dp, None),
            P(dp, None),
            P(every),
            P(dp, TP),
            P(dp, TP),
            P(dp, TP),
            P(TP, dp),
            P(every, None),
            P(dp, None),
        ),
        check_vma=False,
    )
```

```python
import functools

import jax
import jax.numpy as jnp
import numpy as np
from jax import lax
from jax.experimental import pallas as pl
from jax.experimental.pallas import tpu as pltpu
from jax.sharding import Mesh
from jax.sharding import PartitionSpec as P

DK = 128
SEQ = 256
YH, Z, CORES, YL, X = 2, 8, 2, 2, 4
NT = YL * X
TP = ("yl", "x")
F32 = jnp.float32
BF16 = jnp.bfloat16
SWAP = [(0, 1), (1, 0)]


def dot(a, b, ca=1, cb=0):
    return lax.dot_general(a, b, (((ca,), (cb,)), ((), ())), preferred_element_type=F32)


def block_kernel(
    core_ref,
    gain,
    tok_own_h,
    tok_oth_h,
    wq_h,
    cot_own_h,
    cot_oth_h,
    dec_h,
    wo_h,
    enc_h,
    wk_h,
    wv_h,
    buf_h,
    keep,
    send,
    first_up,
    first_down,
    tok,
    cot,
    wq,
    wk,
    wv,
    wo,
    enc,
    dec,
    norm_s,
    norm_t,
    dcode_s,
    q_s,
    k_s,
    v_s,
    dctx_s,
    ctx_s,
    dq_s,
    dk_s,
    dv_s,
    code_s,
    stage,
    rms_s,
    enc_s,
    small_s,
    in_sem,
    out_sem,
):
    width, own = wq.shape
    heads = own // DK
    code = enc.shape[1]
    part = width // (YH * Z)
    core = core_ref[0]
    far = lax.rem(core_ref[1] + Z // 2, Z)
    mine = pl.ds(pl.multiple_of(core * own, own), own)
    pairs = (
        (tok_own_h, tok.at[pl.ds(0, SEQ)]),
        (tok_oth_h, tok.at[pl.ds(SEQ, SEQ)]),
        (wq_h.at[:, mine], wq),
        (wk_h.at[:, mine], wk),
        (wv_h.at[:, mine], wv),
        (cot_own_h, cot.at[pl.ds(0, SEQ)]),
        (cot_oth_h, cot.at[pl.ds(SEQ, SEQ)]),
        (dec_h, dec),
        (wo_h.at[mine, :], wo),
        (enc_h, enc),
    )
    copies = [pltpu.make_async_copy(a, b, in_sem.at[i]) for i, (a, b) in enumerate(pairs)]
    for copy in copies:
        copy.start()

    for s in range(2):
        at = slice(s * SEQ, (s + 1) * SEQ)
        copies[s].wait()
        x = tok[at, :].astype(F32)
        rms = lax.rsqrt(jnp.mean(x * x, axis=-1, keepdims=True) + 1e-6)
        rms_s[at, :] = jnp.broadcast_to(rms, (SEQ, 128))
        norm_s[at, :] = (x * rms * gain[...]).astype(BF16)
    normed = norm_s[...]
    copies[2].wait()
    q_s[...] = dot(normed, wq[...]).astype(BF16)
    norm_t[...] = normed.T
    copies[3].wait()
    k_s[...] = dot(normed, wk[...]).astype(BF16)
    copies[4].wait()
    v_s[...] = dot(normed, wv[...]).astype(BF16)
    for copy in copies[5:]:
        copy.wait()
    dcode_s[...] = dot(cot[...], dec[...], 1, 1).astype(BF16)
    w2 = dot(wo[...], enc[...]).astype(BF16)
    dctx_s[...] = dot(dcode_s[...], w2, 1, 1).astype(BF16)
    scale = DK**-0.5
    row = lax.broadcasted_iota(jnp.int32, (SEQ, SEQ), 0)
    col = lax.broadcasted_iota(jnp.int32, (SEQ, SEQ), 1)
    causal = row <= col
    log2 = scale * 1.4426950408889634
    for s in range(2):
        for h in range(heads):
            at = (slice(s * SEQ, (s + 1) * SEQ), slice(h * DK, (h + 1) * DK))
            q, k, v, dctx = q_s[at], k_s[at], v_s[at], dctx_s[at]
            scores = jnp.where(causal, dot(k, q, 1, 1), -1e30)
            top = jnp.max(scores, axis=0, keepdims=True)
            expo = jnp.exp2((scores - top) * log2)
            probs = expo * (1.0 / jnp.sum(expo, axis=0, keepdims=True))
            low = probs.astype(BF16)
            ctx_s[at] = dot(low, v, 0, 0).astype(BF16)
            dprobs = dot(v, dctx, 1, 1)
            dv_s[at] = dot(low, dctx).astype(BF16)
            delta = jnp.sum(dprobs * probs, axis=0, keepdims=True)
            ds = (probs * (dprobs - delta) * scale).astype(BF16)
            dq_s[at] = dot(ds, k, 0, 0).astype(BF16)
            dk_s[at] = dot(ds, q).astype(BF16)

    def put(i, g):
        lanes = slice(i * own, (i + 1) * own)
        for z in range(Z):
            for y in range(YH):
                at = (y * Z + z) * part
                stage[z, y * part : (y + 1) * part, lanes] = g[at : at + part, :].astype(BF16)
        there = buf_h.at[:, :, pl.ds(i * own, own)]
        copy = pltpu.make_async_copy(stage.at[:, :, pl.ds(i * own, own)], there, out_sem.at[i])
        copy.start()
        return copy

    g = dot(ctx_s[...], dcode_s[...], 0, 0).astype(BF16)
    out = [put(3, dot(enc[...], g, 1, 1))]
    out.append(put(2, dot(norm_t[...], dv_s[...])))
    out.append(put(0, dot(norm_t[...], dq_s[...])))
    out.append(put(1, dot(norm_t[...], dk_s[...])))
    for i in range(2):
        half = YH * part // 2
        (first_up, first_down)[i][...] = stage[far, i * half : (i + 1) * half, :]
    piece = SEQ // NT
    code_s[...] = dot(ctx_s[...], w2).astype(BF16)
    gain_p = jnp.zeros((1, width), F32)
    for s in range(2):
        at = slice(s * SEQ, (s + 1) * SEQ)
        dn = dot(dq_s[at, :], wq[...], 1, 1)
        dn = dn + dot(dk_s[at, :], wk[...], 1, 1)
        dn = dn + dot(dv_s[at, :], wv[...], 1, 1)
        unit = tok[at, :].astype(F32) * rms_s[at, 0:1]
        gain_p = gain_p + jnp.sum(dn * unit, axis=0, keepdims=True)
        low = dn.astype(BF16)
        for t in range(NT):
            here = slice(t * piece, (t + 1) * piece)
            there = slice(s * SEQ + t * piece, s * SEQ + (t + 1) * piece)
            ref = (keep, send)[s]
            ref[t, :, 0:width] = low[here, :]
            ref[t, :, width : width + code] = code_s[there, :]
    enc_s[...] = dot(wo[...], g, 0, 0)
    dec_p = dot(code_s[...], cot[...], 0, 0).astype(BF16)
    n_yz = YH * Z
    fine = part // CORES
    tiny = fine // NT
    rows = code // n_yz // CORES
    cols = width // NT
    blocks = n_yz * rows // piece
    each = piece // rows
    base = width + code
    for cc in range(CORES):
        small = small_s.at[jnp.where(core == cc, 0, 1)]
        for t in range(NT):
            for j in range(blocks):
                dec_at = j * 2 * cols
                dec_b, enc_b = [], []
                for yz in range(j * each, (j + 1) * each):
                    r = (yz * CORES + cc) * rows
                    dec_b.append(dec_p[r : r + rows, t * cols : (t + 1) * cols])
                    e = (yz * CORES + cc) * fine + t * tiny
                    enc_b.append(enc_s[e : e + tiny, 0:cols])
                    enc_b.append(enc_s[e : e + tiny, cols : 2 * cols])
                small[t, :, dec_at : dec_at + cols] = jnp.concatenate(dec_b, axis=0)
                enc_v = jnp.concatenate(enc_b, axis=0).astype(BF16)
                small[t, :, dec_at + cols : dec_at + 2 * cols] = enc_v
    gain_v = jnp.concatenate(
        [gain_p[:, i * 128 : (i + 1) * 128] for i in range(width // 128)]
        + [jnp.zeros((piece - width // 128, 128), F32)],
        axis=0,
    ).astype(BF16)
    end = base + blocks * 2 * cols
    for s, ref in enumerate((keep, send)):
        ref[:, :, base:end] = small_s[s]
        for t in range(NT):
            ref[t, :, end:] = gain_v
    for copy in out:
        copy.wait()


def run_block(core, gain, *args):
    tokens, wq, enc = args[0], args[2], args[7]
    width, own = wq.shape[0], wq.shape[1] // CORES
    code = enc.shape[1]
    part = width // (YH * Z)
    sds = jax.ShapeDtypeStruct
    piece = SEQ // NT
    lanes = width + code + width + 128
    outs = (
        sds((Z, YH * part, 4 * own), BF16),
        sds((NT, piece, lanes), BF16),
        sds((NT, piece, lanes), BF16),
        sds((YH * part // 2, 4 * own), BF16),
        sds((YH * part // 2, 4 * own), BF16),
    )
    vmem = pl.BlockSpec(memory_space=pltpu.VMEM)
    hbm = pl.BlockSpec(memory_space=pl.ANY)
    two = 2 * SEQ
    shapes = (
        (two, width),
        (two, width),
        (width, own),
        (width, own),
        (width, own),
        (own, width),
        (width, code),
        (code, width),
        (two, width),
        (width, two),
        (two, code),
        *(((two, own),) * 8),
        (two, code),
        (Z, YH * part, 4 * own),
    )
    return pl.pallas_call(
        block_kernel,
        in_specs=[pl.BlockSpec(memory_space=pltpu.SMEM), vmem, *([hbm] * len(args))],
        out_specs=[hbm, vmem, vmem, vmem, vmem],
        out_shape=outs,
        scratch_shapes=[
            *(pltpu.VMEM(shape, BF16) for shape in shapes),
            pltpu.VMEM((two, 128), F32),
            pltpu.VMEM((width, code), F32),
            pltpu.VMEM((2, NT, piece, width), BF16),
            pltpu.SemaphoreType.DMA((10,)),
            pltpu.SemaphoreType.DMA((4,)),
        ],
        compiler_params=pltpu.CompilerParams(vmem_limit_bytes=56 * 1024 * 1024),
        cost_estimate=pl.CostEstimate(
            flops=7_500_000_000, bytes_accessed=14_000_000, transcendentals=600_000
        ),
    )(core, gain, *args)


def ring_chunk(buf, z, c, k, sign):
    turn = k * sign * (1 - 2 * c)
    return lax.dynamic_index_in_dim(buf, lax.rem(z + turn + Z, Z), 0, keepdims=False)


def ring_send(a, sign):
    pairs = [
        (at * CORES + core, (at + sign * (1 - 2 * core)) % Z * CORES + core)
        for at in range(Z)
        for core in range(CORES)
    ]
    return lax.ppermute(a, ("z", "c"), pairs)


def ring_add(local, a, sign):
    half = local.shape[0] // 2
    if a.shape[0] == local.shape[0]:
        return (local.astype(F32) + a.astype(F32)).astype(BF16)
    rows = slice(0, half) if sign == 1 else slice(half, 2 * half)
    added = (local[rows].astype(F32) + a.astype(F32)).astype(BF16)
    parts = [added, local[half:]] if sign == 1 else [local[:half], added]
    return jnp.concatenate(parts, axis=0)


def tie(*arrays):
    return lax.optimization_barrier(arrays)


def spread_kernel(core_ref, here, away, *outs):
    own = outs[0].shape[1] // CORES
    core = core_ref[0]
    for ref, at in ((here, core), (away, 1 - core)):
        lanes = pl.ds(pl.multiple_of(at * own, own), own)
        for i, out in enumerate(outs):
            out[:, lanes] = ref[:, i * own : (i + 1) * own].astype(F32)


def spread(core, here, away):
    rows, own = here.shape[0], here.shape[1] // 4
    vmem = pl.BlockSpec(memory_space=pltpu.VMEM)
    return pl.pallas_call(
        spread_kernel,
        in_specs=[pl.BlockSpec(memory_space=pltpu.SMEM), vmem, vmem],
        out_specs=[vmem] * 4,
        out_shape=[jax.ShapeDtypeStruct((rows, CORES * own), F32)] * 4,
        compiler_params=pltpu.CompilerParams(vmem_limit_bytes=16 * 1024 * 1024),
    )(core, here, away)


def on_device(tokens, gain, w_query, w_key, w_value, w_output, encoder, decoder, cotangent):
    rows, width = tokens.shape
    own = w_query.shape[1] // CORES
    code_w = encoder.shape[1]
    yh, z, c = lax.axis_index("yh"), lax.axis_index("z"), lax.axis_index("c")
    t = lax.axis_index("yl") * X + lax.axis_index("x")
    n_dp = YH * Z * CORES
    fine = width // n_dp
    tiny = fine // NT
    core = jnp.stack([c, z]).astype(jnp.int32)

    tok_oth = lax.ppermute(tokens, "c", SWAP)
    cot_oth = lax.ppermute(cotangent, "c", SWAP)
    buf, keep, send, first_up, first_down = run_block(
        core,
        gain.reshape(1, width),
        tokens,
        tok_oth,
        w_query,
        cotangent,
        cot_oth,
        decoder,
        w_output,
        encoder,
        w_key,
        w_value,
    )
    chunk = functools.partial(ring_chunk, buf, z, c)
    up = ring_send(first_up, 1)
    down = ring_send(first_down, -1)
    both = (keep.astype(F32) + lax.ppermute(send, "c", SWAP).astype(F32)).astype(BF16)
    up, _ = tie(up, both)
    up = ring_add(chunk(3, 1), up, 1)
    up, down = tie(up, down)
    over_t = lax.all_to_all(both, TP, 0, 0, tiled=True)
    up = ring_send(up, 1)
    down = ring_send(ring_add(chunk(3, -1), down, -1), -1)
    total = jnp.sum(over_t.astype(F32), axis=0)
    piece = rows // NT
    out_w = width + code_w
    cols = width // NT
    dec_rows = code_w // n_dp
    small = total[:, out_w : out_w + width]
    small = jnp.concatenate(
        [small[:, i * 2 * cols : (i + 1) * 2 * cols] for i in range(width // (2 * cols))], axis=0
    ).reshape(YH * Z, dec_rows, 2 * cols)
    gain_v = total[: width // 128, out_w + width :]
    small = jnp.concatenate(
        [small, jnp.broadcast_to(gain_v[None], (YH * Z, *gain_v.shape))], axis=2
    ).astype(BF16)
    small, up = tie(small, up)
    small = lax.all_to_all(small, ("yh", "z"), 0, 0, tiled=True)
    up = ring_add(chunk(2, 1), up, 1)
    up, down = tie(up, down)
    up = ring_send(up, 1)
    down = ring_send(ring_add(chunk(2, -1), down, -1), -1)
    up = ring_add(chunk(1, 1), up, 1)
    up, down = tie(up, down)
    up = ring_send(up, 1)

    dnormed = total[:, :width]
    x = lax.dynamic_slice_in_dim(tokens, t * piece, piece, 0).astype(F32)
    cot = lax.dynamic_slice_in_dim(cotangent, t * piece, piece, 0).astype(F32)
    rms = lax.rsqrt(jnp.mean(x * x, axis=-1, keepdims=True) + 1e-6)
    unit = x * rms
    dunit = dnormed * gain
    inner = jnp.sum(dunit * unit, axis=-1, keepdims=True) / width
    grad_rows = cot + rms * (dunit - unit * inner)
    mine = jnp.concatenate([grad_rows, total[:, width:out_w]], axis=1).astype(BF16)

    small = jnp.sum(small.astype(F32), axis=0)
    enc_v = small[:, cols : 2 * cols]
    grad_encoder = jnp.concatenate([enc_v[:tiny], enc_v[tiny:]], axis=1)
    at = (((yh * Z + z) * CORES + c) * NT + t) * tiny
    grad_gain = lax.dynamic_slice(small, (at // 128, 2 * cols + at % 128), (1, tiny))[0]

    dec_b = jnp.pad(small[:, :cols].astype(BF16), ((0, piece - dec_rows), (0, 0)))
    mine = jnp.concatenate([mine, dec_b], axis=1)
    over_t = lax.all_to_all(
        jnp.broadcast_to(mine[None], (NT, *mine.shape)), TP, 0, 0, tiled=True
    )
    down = ring_send(ring_add(chunk(1, -1), down, -1), -1)
    red = (chunk(0, 1).astype(F32) + up.astype(F32) + down.astype(F32)).astype(BF16)
    whole_rows = over_t[:, :, :out_w].reshape(rows, out_w)
    grad_input = whole_rows[:, :width]
    output = (tokens.astype(F32) + dot(whole_rows[:, width:], decoder)).astype(BF16)
    grad_decoder = over_t[:, :dec_rows, out_w:].astype(F32)
    grad_decoder = grad_decoder.transpose(1, 0, 2).reshape(dec_rows, width)

    red = red.reshape(YH, CORES * fine, 4 * own)
    away = lax.dynamic_index_in_dim(red, 1 - yh, 0, keepdims=False)
    here = lax.dynamic_index_in_dim(red, yh, 0, keepdims=False)
    both = here.astype(F32) + lax.ppermute(away, "yh", SWAP).astype(F32)
    both = both.astype(BF16).reshape(CORES, fine, 4 * own)
    here = lax.dynamic_index_in_dim(both, c, 0, keepdims=False)
    away = lax.dynamic_index_in_dim(both, 1 - c, 0, keepdims=False)
    away = lax.ppermute(away, "c", SWAP)
    grads = spread(core, here, away)

    return (
        output,
        grad_input,
        grad_gain,
        grads[0],
        grads[1],
        grads[2],
        grads[3].T,
        grad_encoder,
        grad_decoder,
    )


def solution(mesh):
    devices = np.asarray(mesh.devices).reshape(YH, Z, CORES, YL, X)
    fine = Mesh(devices, ("yh", "z", "c", "yl", "x"))
    dp = ("yh", "z", "c")
    every = (*dp, *TP)
    return jax.shard_map(
        on_device,
        mesh=fine,
        in_specs=(
            P(dp, None),
            P(),
            P(None, TP),
            P(None, TP),
            P(None, TP),
            P(TP, None),
            P(),
            P(),
            P(dp, None),
        ),
        out_specs=(
            P(dp, None),
            P(dp, None),
            P(every),
            P(dp, TP),
            P(dp, TP),
            P(dp, TP),
            P(TP, dp),
            P(every, None),
            P(dp, None),
        ),
        check_vma=False,
    )
```

```python
import functools

import jax
import jax.numpy as jnp
import numpy as np
from jax import lax
from jax.experimental import pallas as pl
from jax.experimental.pallas import tpu as pltpu
from jax.sharding import Mesh
from jax.sharding import PartitionSpec as P

DK = 128
SEQ = 256
YH, Z, CORES, YL, X = 2, 8, 2, 2, 4
NT = YL * X
TP = ("yl", "x")
F32 = jnp.float32
BF16 = jnp.bfloat16
SWAP = [(0, 1), (1, 0)]


def dot(a, b, ca=1, cb=0):
    return lax.dot_general(a, b, (((ca,), (cb,)), ((), ())), preferred_element_type=F32)


def block_kernel(
    core_ref,
    gain,
    tok_own_h,
    tok_oth_h,
    wq_h,
    cot_own_h,
    cot_oth_h,
    dec_h,
    wo_h,
    enc_h,
    wk_h,
    wv_h,
    buf_h,
    keep,
    send,
    first_up,
    first_down,
    tok,
    cot,
    wq,
    wk,
    wv,
    wo,
    enc,
    dec,
    norm_s,
    norm_t,
    dcode_s,
    q_s,
    k_s,
    v_s,
    dctx_s,
    ctx_s,
    dq_s,
    dk_s,
    dv_s,
    code_s,
    stage,
    rms_s,
    enc_s,
    small_s,
    in_sem,
    out_sem,
):
    width, own = wq.shape
    heads = own // DK
    code = enc.shape[1]
    part = width // (YH * Z)
    core = core_ref[0]
    far = lax.rem(core_ref[1] + Z // 2, Z)
    mine = pl.ds(pl.multiple_of(core * own, own), own)
    pairs = (
        (tok_own_h, tok.at[pl.ds(0, SEQ)]),
        (tok_oth_h, tok.at[pl.ds(SEQ, SEQ)]),
        (wq_h.at[:, mine], wq),
        (wk_h.at[:, mine], wk),
        (wv_h.at[:, mine], wv),
        (cot_own_h, cot.at[pl.ds(0, SEQ)]),
        (cot_oth_h, cot.at[pl.ds(SEQ, SEQ)]),
        (dec_h, dec),
        (wo_h.at[mine, :], wo),
        (enc_h, enc),
    )
    copies = [pltpu.make_async_copy(a, b, in_sem.at[i]) for i, (a, b) in enumerate(pairs)]
    for copy in copies:
        copy.start()

    for s in range(2):
        at = slice(s * SEQ, (s + 1) * SEQ)
        copies[s].wait()
        x = tok[at, :].astype(F32)
        rms = lax.rsqrt(jnp.mean(x * x, axis=-1, keepdims=True) + 1e-6)
        rms_s[at, :] = jnp.broadcast_to(rms, (SEQ, 128))
        norm_s[at, :] = (x * rms * gain[...]).astype(BF16)
    normed = norm_s[...]
    copies[2].wait()
    q_s[...] = dot(normed, wq[...]).astype(BF16)
    norm_t[...] = normed.T
    copies[3].wait()
    k_s[...] = dot(normed, wk[...]).astype(BF16)
    copies[4].wait()
    v_s[...] = dot(normed, wv[...]).astype(BF16)
    for copy in copies[5:]:
        copy.wait()
    dcode_s[...] = dot(cot[...], dec[...], 1, 1).astype(BF16)
    w2 = dot(wo[...], enc[...]).astype(BF16)
    dctx_s[...] = dot(dcode_s[...], w2, 1, 1).astype(BF16)
    scale = DK**-0.5
    row = lax.broadcasted_iota(jnp.int32, (SEQ, SEQ), 0)
    col = lax.broadcasted_iota(jnp.int32, (SEQ, SEQ), 1)
    causal = row <= col
    log2 = scale * 1.4426950408889634
    for s in range(2):
        for h in range(heads):
            at = (slice(s * SEQ, (s + 1) * SEQ), slice(h * DK, (h + 1) * DK))
            q, k, v, dctx = q_s[at], k_s[at], v_s[at], dctx_s[at]
            scores = jnp.where(causal, dot(k, q, 1, 1), -1e30)
            top = jnp.max(scores, axis=0, keepdims=True)
            expo = jnp.exp2((scores - top) * log2)
            probs = expo * (1.0 / jnp.sum(expo, axis=0, keepdims=True))
            low = probs.astype(BF16)
            ctx_s[at] = dot(low, v, 0, 0).astype(BF16)
            dprobs = dot(v, dctx, 1, 1)
            dv_s[at] = dot(low, dctx).astype(BF16)
            delta = jnp.sum(dprobs * probs, axis=0, keepdims=True)
            ds = (probs * (dprobs - delta) * scale).astype(BF16)
            dq_s[at] = dot(ds, k, 0, 0).astype(BF16)
            dk_s[at] = dot(ds, q).astype(BF16)

    def put(i, g):
        lanes = slice(i * own, (i + 1) * own)
        for z in range(Z):
            for y in range(YH):
                at = (y * Z + z) * part
                stage[z, y * part : (y + 1) * part, lanes] = g[at : at + part, :].astype(BF16)
        there = buf_h.at[:, :, pl.ds(i * own, own)]
        copy = pltpu.make_async_copy(stage.at[:, :, pl.ds(i * own, own)], there, out_sem.at[i])
        copy.start()
        return copy

    g = dot(ctx_s[...], dcode_s[...], 0, 0).astype(BF16)
    out = [put(3, dot(enc[...], g, 1, 1))]
    out.append(put(2, dot(norm_t[...], dv_s[...])))
    out.append(put(0, dot(norm_t[...], dq_s[...])))
    out.append(put(1, dot(norm_t[...], dk_s[...])))
    for i in range(2):
        half = YH * part // 2
        (first_up, first_down)[i][...] = stage[far, i * half : (i + 1) * half, :]
    piece = SEQ // NT
    code_s[...] = dot(ctx_s[...], w2).astype(BF16)
    gain_p = jnp.zeros((1, width), F32)
    for s in range(2):
        at = slice(s * SEQ, (s + 1) * SEQ)
        dn = dot(dq_s[at, :], wq[...], 1, 1)
        dn = dn + dot(dk_s[at, :], wk[...], 1, 1)
        dn = dn + dot(dv_s[at, :], wv[...], 1, 1)
        unit = tok[at, :].astype(F32) * rms_s[at, 0:1]
        gain_p = gain_p + jnp.sum(dn * unit, axis=0, keepdims=True)
        low = dn.astype(BF16)
        for t in range(NT):
            here = slice(t * piece, (t + 1) * piece)
            there = slice(s * SEQ + t * piece, s * SEQ + (t + 1) * piece)
            ref = (keep, send)[s]
            ref[t, :, 0:width] = low[here, :]
            ref[t, :, width : width + code] = code_s[there, :]
    enc_s[...] = dot(wo[...], g, 0, 0)
    dec_p = dot(code_s[...], cot[...], 0, 0).astype(BF16)
    n_yz = YH * Z
    fine = part // CORES
    tiny = fine // NT
    rows = code // n_yz // CORES
    cols = width // NT
    blocks = n_yz * rows // piece
    each = piece // rows
    base = width + code
    for cc in range(CORES):
        small = small_s.at[jnp.where(core == cc, 0, 1)]
        for t in range(NT):
            for j in range(blocks):
                dec_at = j * 2 * cols
                dec_b, enc_b = [], []
                for yz in range(j * each, (j + 1) * each):
                    r = (yz * CORES + cc) * rows
                    dec_b.append(dec_p[r : r + rows, t * cols : (t + 1) * cols])
                    e = (yz * CORES + cc) * fine + t * tiny
                    enc_b.append(enc_s[e : e + tiny, 0:cols])
                    enc_b.append(enc_s[e : e + tiny, cols : 2 * cols])
                small[t, :, dec_at : dec_at + cols] = jnp.concatenate(dec_b, axis=0)
                enc_v = jnp.concatenate(enc_b, axis=0).astype(BF16)
                small[t, :, dec_at + cols : dec_at + 2 * cols] = enc_v
    gain_v = jnp.concatenate(
        [gain_p[:, i * 128 : (i + 1) * 128] for i in range(width // 128)]
        + [jnp.zeros((piece - width // 128, 128), F32)],
        axis=0,
    ).astype(BF16)
    end = base + blocks * 2 * cols
    for s, ref in enumerate((keep, send)):
        ref[:, :, base:end] = small_s[s]
        for t in range(NT):
            ref[t, :, end:] = gain_v
    for copy in out:
        copy.wait()


def run_block(core, gain, *args):
    tokens, wq, enc = args[0], args[2], args[7]
    width, own = wq.shape[0], wq.shape[1] // CORES
    code = enc.shape[1]
    part = width // (YH * Z)
    sds = jax.ShapeDtypeStruct
    piece = SEQ // NT
    lanes = width + code + width + 128
    outs = (
        sds((Z, YH * part, 4 * own), BF16),
        sds((NT, piece, lanes), BF16),
        sds((NT, piece, lanes), BF16),
        sds((YH * part // 2, 4 * own), BF16),
        sds((YH * part // 2, 4 * own), BF16),
    )
    vmem = pl.BlockSpec(memory_space=pltpu.VMEM)
    hbm = pl.BlockSpec(memory_space=pl.ANY)
    two = 2 * SEQ
    shapes = (
        (two, width),
        (two, width),
        (width, own),
        (width, own),
        (width, own),
        (own, width),
        (width, code),
        (code, width),
        (two, width),
        (width, two),
        (two, code),
        *(((two, own),) * 8),
        (two, code),
        (Z, YH * part, 4 * own),
    )
    return pl.pallas_call(
        block_kernel,
        in_specs=[pl.BlockSpec(memory_space=pltpu.SMEM), vmem, *([hbm] * len(args))],
        out_specs=[hbm, vmem, vmem, vmem, vmem],
        out_shape=outs,
        scratch_shapes=[
            *(pltpu.VMEM(shape, BF16) for shape in shapes),
            pltpu.VMEM((two, 128), F32),
            pltpu.VMEM((width, code), F32),
            pltpu.VMEM((2, NT, piece, width), BF16),
            pltpu.SemaphoreType.DMA((10,)),
            pltpu.SemaphoreType.DMA((4,)),
        ],
        compiler_params=pltpu.CompilerParams(vmem_limit_bytes=56 * 1024 * 1024),
        cost_estimate=pl.CostEstimate(
            flops=7_500_000_000, bytes_accessed=14_000_000, transcendentals=600_000
        ),
    )(core, gain, *args)


def ring_chunk(buf, z, c, k, sign):
    turn = k * sign * (1 - 2 * c)
    return lax.dynamic_index_in_dim(buf, lax.rem(z + turn + Z, Z), 0, keepdims=False)


def ring_send(a, sign):
    pairs = [
        (at * CORES + core, (at + sign * (1 - 2 * core)) % Z * CORES + core)
        for at in range(Z)
        for core in range(CORES)
    ]
    return lax.ppermute(a, ("z", "c"), pairs)


def ring_add(local, a, sign):
    half = local.shape[0] // 2
    if a.shape[0] == local.shape[0]:
        return (local.astype(F32) + a.astype(F32)).astype(BF16)
    rows = slice(0, half) if sign == 1 else slice(half, 2 * half)
    added = (local[rows].astype(F32) + a.astype(F32)).astype(BF16)
    parts = [added, local[half:]] if sign == 1 else [local[:half], added]
    return jnp.concatenate(parts, axis=0)


def tie(*arrays):
    return lax.optimization_barrier(arrays)


def spread_kernel(core_ref, here, away, *outs):
    own = outs[0].shape[1] // CORES
    core = core_ref[0]
    for ref, at in ((here, core), (away, 1 - core)):
        lanes = pl.ds(pl.multiple_of(at * own, own), own)
        for i, out in enumerate(outs):
            out[:, lanes] = ref[:, i * own : (i + 1) * own].astype(F32)


def spread(core, here, away):
    rows, own = here.shape[0], here.shape[1] // 4
    vmem = pl.BlockSpec(memory_space=pltpu.VMEM)
    return pl.pallas_call(
        spread_kernel,
        in_specs=[pl.BlockSpec(memory_space=pltpu.SMEM), vmem, vmem],
        out_specs=[vmem] * 4,
        out_shape=[jax.ShapeDtypeStruct((rows, CORES * own), F32)] * 4,
        compiler_params=pltpu.CompilerParams(vmem_limit_bytes=16 * 1024 * 1024),
    )(core, here, away)


def on_device(tokens, gain, w_query, w_key, w_value, w_output, encoder, decoder, cotangent):
    rows, width = tokens.shape
    own = w_query.shape[1] // CORES
    code_w = encoder.shape[1]
    yh, z, c = lax.axis_index("yh"), lax.axis_index("z"), lax.axis_index("c")
    t = lax.axis_index("yl") * X + lax.axis_index("x")
    n_dp = YH * Z * CORES
    fine = width // n_dp
    tiny = fine // NT
    core = jnp.stack([c, z]).astype(jnp.int32)

    tok_oth = lax.ppermute(tokens, "c", SWAP)
    cot_oth = lax.ppermute(cotangent, "c", SWAP)
    buf, keep, send, first_up, first_down = run_block(
        core,
        gain.reshape(1, width),
        tokens,
        tok_oth,
        w_query,
        cotangent,
        cot_oth,
        decoder,
        w_output,
        encoder,
        w_key,
        w_value,
    )
    chunk = functools.partial(ring_chunk, buf, z, c)
    up = ring_send(first_up, 1)
    down = ring_send(first_down, -1)
    both = (keep.astype(F32) + lax.ppermute(send, "c", SWAP).astype(F32)).astype(BF16)
    up = ring_add(chunk(3, 1), up, 1)
    up, down = tie(up, down)
    over_t = lax.all_to_all(both, TP, 0, 0, tiled=True)
    up = ring_send(up, 1)
    down = ring_send(ring_add(chunk(3, -1), down, -1), -1)
    total = jnp.sum(over_t.astype(F32), axis=0)
    piece = rows // NT
    out_w = width + code_w
    cols = width // NT
    dec_rows = code_w // n_dp
    small = total[:, out_w : out_w + width]
    small = jnp.concatenate(
        [small[:, i * 2 * cols : (i + 1) * 2 * cols] for i in range(width // (2 * cols))], axis=0
    ).reshape(YH * Z, dec_rows, 2 * cols)
    gain_v = total[: width // 128, out_w + width :]
    small = jnp.concatenate(
        [small, jnp.broadcast_to(gain_v[None], (YH * Z, *gain_v.shape))], axis=2
    ).astype(BF16)
    small, up = tie(small, up)
    small = lax.all_to_all(small, ("yh", "z"), 0, 0, tiled=True)
    up = ring_add(chunk(2, 1), up, 1)
    up, down = tie(up, down)
    up = ring_send(up, 1)
    down = ring_send(ring_add(chunk(2, -1), down, -1), -1)
    up = ring_add(chunk(1, 1), up, 1)
    up, down = tie(up, down)
    up = ring_send(up, 1)

    dnormed = total[:, :width]
    x = lax.dynamic_slice_in_dim(tokens, t * piece, piece, 0).astype(F32)
    cot = lax.dynamic_slice_in_dim(cotangent, t * piece, piece, 0).astype(F32)
    rms = lax.rsqrt(jnp.mean(x * x, axis=-1, keepdims=True) + 1e-6)
    unit = x * rms
    dunit = dnormed * gain
    inner = jnp.sum(dunit * unit, axis=-1, keepdims=True) / width
    grad_rows = cot + rms * (dunit - unit * inner)
    mine = jnp.concatenate([grad_rows, total[:, width:out_w]], axis=1).astype(BF16)

    small = jnp.sum(small.astype(F32), axis=0)
    enc_v = small[:, cols : 2 * cols]
    grad_encoder = jnp.concatenate([enc_v[:tiny], enc_v[tiny:]], axis=1)
    at = (((yh * Z + z) * CORES + c) * NT + t) * tiny
    grad_gain = lax.dynamic_slice(small, (at // 128, 2 * cols + at % 128), (1, tiny))[0]

    dec_b = jnp.pad(small[:, :cols].astype(BF16), ((0, piece - dec_rows), (0, 0)))
    mine = jnp.concatenate([mine, dec_b], axis=1)
    over_t = lax.all_to_all(
        jnp.broadcast_to(mine[None], (NT, *mine.shape)), TP, 0, 0, tiled=True
    )
    down = ring_send(ring_add(chunk(1, -1), down, -1), -1)
    red = (chunk(0, 1).astype(F32) + up.astype(F32) + down.astype(F32)).astype(BF16)
    whole_rows = over_t[:, :, :out_w].reshape(rows, out_w)
    grad_input = whole_rows[:, :width]
    output = (tokens.astype(F32) + dot(whole_rows[:, width:], decoder)).astype(BF16)
    grad_decoder = over_t[:, :dec_rows, out_w:].astype(F32)
    grad_decoder = grad_decoder.transpose(1, 0, 2).reshape(dec_rows, width)

    red = red.reshape(YH, CORES * fine, 4 * own)
    away = lax.dynamic_index_in_dim(red, 1 - yh, 0, keepdims=False)
    here = lax.dynamic_index_in_dim(red, yh, 0, keepdims=False)
    both = here.astype(F32) + lax.ppermute(away, "yh", SWAP).astype(F32)
    both = both.astype(BF16).reshape(CORES, fine, 4 * own)
    here = lax.dynamic_index_in_dim(both, c, 0, keepdims=False)
    away = lax.dynamic_index_in_dim(both, 1 - c, 0, keepdims=False)
    away = lax.ppermute(away, "c", SWAP)
    grads = spread(core, here, away)

    return (
        output,
        grad_input,
        grad_gain,
        grads[0],
        grads[1],
        grads[2],
        grads[3].T,
        grad_encoder,
        grad_decoder,
    )


def solution(mesh):
    devices = np.asarray(mesh.devices).reshape(YH, Z, CORES, YL, X)
    fine = Mesh(devices, ("yh", "z", "c", "yl", "x"))
    dp = ("yh", "z", "c")
    every = (*dp, *TP)
    return jax.shard_map(
        on_device,
        mesh=fine,
        in_specs=(
            P(dp, None),
            P(),
            P(None, TP),
            P(None, TP),
            P(None, TP),
            P(TP, None),
            P(),
            P(),
            P(dp, None),
        ),
        out_specs=(
            P(dp, None),
            P(dp, None),
            P(every),
            P(dp, TP),
            P(dp, TP),
            P(dp, TP),
            P(TP, dp),
            P(every, None),
            P(dp, None),
        ),
        check_vma=False,
    )
```
